256 devices in a mesh: row: 16 (over x, z_lo), col: 16 (over y, z_hi, core).
Axes of the slice: x: 4, y: 4, z: 8 (z_hi: 2, z_lo: 4; z = z_hi * 4 + z_lo), core: 2. Of those that a mesh axis runs over, the one named last changes fastest.
Arguments:
- noise: bfloat16 [6144, 4096], P('row', 'col'), may hold values from -8 to 8
- data: bfloat16 [8192, 4096], P('col', 'row'), may hold values from -6 to 6
Outputs:
- targets: bfloat16 [6144, 4096], P('row', 'col')
- row_potential: float32 [6144], P('row')
- col_potential: float32 [8192], P('col')
The draws below stay inside these ranges and needn't reach their ends.
All inputs are finite; a program needn't handle non-finite values.
Results may differ from the reference program's by a relative error of at most 0.018.
Values may be sent and summed in bfloat16 or wider, within the bound.
A program may use at most 64 MiB of HBM per device.

```python
import jax
import jax.numpy as jnp

F = 4096
ITERS = 3
NOISE = 6144
DATA = 8192


def draw_noise(key, part):
    key = jax.random.fold_in(key, 7)
    values = jax.random.normal(key, (NOISE, F), jnp.float32)
    return jnp.clip(values, -8.0, 8.0).astype(jnp.bfloat16)


def level_of(stream_key, dims, shards, least, high):
    def one(position, blocks):
        steps = jax.random.uniform(jax.random.fold_in(jax.random.fold_in(stream_key, 6), position), (blocks,), jnp.float32, least / len(shards), high / len(shards))
        return jnp.repeat(jnp.exp(steps), dims[position] // blocks).reshape((-1,) + (1,) * (len(dims) - position - 1))

    level = one(*shards[0])
    for cut in shards[1:]:
        level = level * one(*cut)
    return level


def normal_values(key, extent, deviation, reach, cuts=(), dtype=jnp.bfloat16):
    loudness = level_of(key, extent, cuts, -0.22, 0.18) if cuts else 1.0
    drawn = jax.random.normal(key, extent, jnp.float32) * deviation * loudness
    return jnp.minimum(jnp.maximum(drawn, -reach), reach).astype(dtype)


def setup_inputs(seed: int = 0) -> dict:
    key_list = jax.random.split(jax.random.key(seed), 3)
    return {
        "noise": draw_noise(jax.random.fold_in(key_list[2], 71), 0),
        "data": normal_values(key_list[1], (DATA, F), 1.0, 6.0, ((0, 16), (1, 16))),
    }


EPS = 0.01


def log_mean_exp(scores, axis, count):
    top = jnp.max(scores, axis=axis, keepdims=True)
    total = jnp.sum(jnp.exp(scores - top), axis=axis)
    return jnp.squeeze(top, axis) + jnp.log(total / count)


def reference(noise, data):
    cross = jnp.dot(noise, data.T, preferred_element_type=jnp.float32)
    noise_sq = jnp.sum(jnp.square(noise.astype(jnp.float32)), axis=1)
    data_sq = jnp.sum(jnp.square(data.astype(jnp.float32)), axis=1)
    cost = (noise_sq[:, None] + data_sq[None, :] - 2.0 * cross) / F
    col_potential = jnp.zeros((DATA,), jnp.float32)
    for step in range(ITERS):
        row_potential = -EPS * log_mean_exp((col_potential[None, :] - cost) / EPS, 1, DATA)
        col_potential = -EPS * log_mean_exp((row_potential[:, None] - cost) / EPS, 0, NOISE)
    row_potential = -EPS * log_mean_exp((col_potential[None, :] - cost) / EPS, 1, DATA)
    plan = (jnp.exp((row_potential[:, None] + col_potential[None, :] - cost) / EPS) / DATA).astype(jnp.bfloat16)
    targets = jnp.dot(plan, data, preferred_element_type=jnp.float32).astype(jnp.bfloat16)
    return targets, row_potential, col_potential
```

```python
import functools
import math

import jax
import jax.numpy as jnp
from jax import lax
from jax.experimental import pallas as pl
from jax.experimental.pallas import tpu as pltpu
from jax.sharding import PartitionSpec as P

ITERS = 3
EPS = 0.01
LOG2E = math.log2(math.e)
MESH = pl.DeviceIdType.MESH
NT = (((1,), (1,)), ((), ()))
LANES = 128


def eye():
    r = lax.broadcasted_iota(jnp.int32, (LANES, LANES), 0)
    c = lax.broadcasted_iota(jnp.int32, (LANES, LANES), 1)
    return r == c


def to_lanes(column, mask):
    return jnp.sum(jnp.where(mask, column, 0.0), axis=0, keepdims=True)


def to_sublanes(line, mask):
    return jnp.sum(jnp.where(mask, line, 0.0), axis=1, keepdims=True)


def kernel(
    width,
    noise_ref,
    data_ref,
    targets_ref,
    row_ref,
    col_ref,
    noise_all,
    data_all,
    scores,
    plan,
    u_col,
    u_line,
    v_line,
    top_col,
    noise_sq,
    data_sq,
    row_box,
    col_box,
    to_twin,
    from_twin,
    own,
    relay_out,
    relay_in,
    pair_out,
    pair_in,
    z_out,
    z_in,
    send_sem,
    recv_sem,
    box_send,
    box_recv,
):
    rows, part = noise_ref.shape
    cols = data_ref.shape[0]
    n_row, n_col = 16, 16
    row, col = lax.axis_index("row"), lax.axis_index("col")
    x, zl = row // 4, row % 4
    y, zh, core = col // 4, (col // 2) % 2, col % 2
    mask = eye()
    started = []

    def row_of(x_, zl_):
        return x_ * 4 + zl_

    def col_of(y_, zh_, core_):
        return (y_ * 2 + zh_) * 2 + core_

    def send(src, dst, to):
        n = len(started)
        copy = pltpu.make_async_remote_copy(
            src_ref=src,
            dst_ref=dst,
            send_sem=send_sem.at[n],
            recv_sem=recv_sem.at[n],
            device_id=to,
            device_id_type=MESH,
        )
        copy.start()
        started.append(copy)
        return copy

    barrier = pltpu.get_barrier_semaphore()

    def greet(d, carry):
        pl.semaphore_signal(barrier, inc=1, device_id=(lax.rem(row + d, n_row), col), device_id_type=MESH)
        pl.semaphore_signal(barrier, inc=1, device_id=(row, lax.rem(col + d, n_col)), device_id_type=MESH)
        return carry

    lax.fori_loop(1, 16, greet, 0)
    noise_all[col] = noise_ref[...]
    data_all[row] = data_ref[...]
    pl.semaphore_wait(barrier, 30)

    x_next, x_prev = lax.rem(x + 1, 4), lax.rem(x + 3, 4)
    y_next, y_prev = lax.rem(y + 1, 4), lax.rem(y + 3, 4)
    x_far, y_far = lax.rem(x + 2, 4), lax.rem(y + 2, 4)
    zls = (zl, zl + 1 - 2 * lax.rem(zl, 2), lax.rem(zl + 2, 4), 3 - zl)
    half_d, half_n = cols // 2, rows // 2
    twin = (row, col_of(y, zh, 1 - core))
    partner = (row, col_of(y, 1 - zh, core))

    def data_x(j):
        block = data_all.at[row_of(x, zls[j])]
        return (
            send(block, block, (row_of(x_next, zl), col)),
            send(block, block, (row_of(x_prev, zl), col)),
        )

    def data_x_on(j):
        a = data_all.at[row_of(x_prev, zls[j]), pl.ds(0, half_d)]
        b = data_all.at[row_of(x_next, zls[j]), pl.ds(half_d, half_d)]
        from_prev, from_next = near[j]
        from_prev.wait_recv()
        fa = send(a, a, (row_of(x_next, zl), col))
        from_next.wait_recv()
        fb = send(b, b, (row_of(x_prev, zl), col))
        return fa, fb

    def noise_y(z_):
        block = noise_all.at[col_of(y, z_, core)]
        return (
            send(block, block, (row, col_of(y_next, zh, core))),
            send(block, block, (row, col_of(y_prev, zh, core))),
        )

    def to_the_twin(y_, z_):
        block = noise_all.at[col_of(y_, z_, core)]
        twins.append(send(block, block, twin))

    def noise_y_on(z_, pair):
        a = noise_all.at[col_of(y_prev, z_, core), pl.ds(0, half_n)]
        b = noise_all.at[col_of(y_next, z_, core), pl.ds(half_n, half_n)]
        pair[0].wait_recv()
        fa = send(a, a, (row, col_of(y_next, zh, core)))
        pair[1].wait_recv()
        fb = send(b, b, (row, col_of(y_prev, zh, core)))
        to_the_twin(y_prev, z_)
        to_the_twin(y_next, z_)
        return fa, fb

    twins, near, far = [], [], []
    own_noise, own_data = noise_all.at[col], data_all.at[row]
    cross_z = send(own_noise, own_noise, partner)
    z_line = [None] + [send(own_data, own_data, (row_of(x, zls[j]), col)) for j in (1, 2, 3)]
    near.append(data_x(0))
    near_n = noise_y(zh)
    to_the_twin(y, zh)

    z_line[1].wait_recv()
    near.append(data_x(1))
    far.append(data_x_on(0))
    far_n = noise_y_on(zh, near_n)
    cross_z.wait_recv()
    near_o = noise_y(1 - zh)
    to_the_twin(y, 1 - zh)
    z_line[2].wait_recv()
    near.append(data_x(2))
    far.append(data_x_on(1))
    z_line[3].wait_recv()
    near.append(data_x(3))
    far_o = noise_y_on(1 - zh, near_o)
    far_n[0].wait_recv()
    far_n[1].wait_recv()
    to_the_twin(y_far, zh)
    far.append(data_x_on(2))
    far_o[0].wait_recv()
    far_o[1].wait_recv()
    to_the_twin(y_far, 1 - zh)
    far.append(data_x_on(3))
    for t in twins:
        t.wait_recv()
    for a, b in far:
        a.wait_recv()
        b.wait_recv()

    scores[...] = jnp.zeros_like(scores)
    noise_sq[...] = jnp.zeros_like(noise_sq)
    data_sq[...] = jnp.zeros_like(data_sq)

    def accumulate(k, carry):
        a, b = noise_all[k], data_all[k]
        scores[...] += lax.dot_general(a, b, NT, preferred_element_type=jnp.float32)
        a, b = a.astype(jnp.float32), b.astype(jnp.float32)
        a, b = a * a, b * b
        noise_sq[...] += a[:, :LANES] + a[:, LANES:]
        data_sq[...] += b[:, :LANES] + b[:, LANES:]
        return carry

    lax.fori_loop(0, 16, accumulate, 0)
    unit = LOG2E / (EPS * width)
    for i in range(0, rows, LANES):
        scores[i : i + LANES, :] = scores[i : i + LANES, :] * (2.0 * unit)
    for j in range(0, cols, LANES):
        s = to_lanes(jnp.sum(data_sq[j : j + LANES, :], axis=1, keepdims=True), mask)
        col_ref[:, j : j + LANES] = s
        v_line[:, j : j + LANES] = s * -unit

    def share(box, mine, peer_of):
        def one(d, carry):
            pltpu.make_async_remote_copy(
                src_ref=box.at[mine],
                dst_ref=box.at[mine],
                send_sem=box_send.at[shared[0]],
                recv_sem=box_recv.at[shared[0]],
                device_id=peer_of(d),
                device_id_type=MESH,
            ).start()
            return carry

        lax.fori_loop(1, 16, one, 0)

    def settle(box):
        n = shared[0]
        shared[0] += 1
        many = box.at[pl.ds(0, 15)]
        pltpu.make_async_copy(many, many, box_recv.at[n]).wait()
        pltpu.make_async_copy(many, many, box_send.at[n]).wait()

    shared = [0]

    def row_peer(d):
        return (row, lax.rem(col + d, n_col))

    def col_peer(d):
        return (lax.rem(row + d, n_row), col)

    def merge(box, count):
        lines = box[...]
        top = jnp.max(lines, axis=0)
        total = jnp.sum(jnp.exp2(lines - top[None]), axis=0)
        return top + jnp.log(total / count) * LOG2E

    def row_local(box, last):
        v = v_line[...]
        for i in range(0, rows, LANES):
            s = scores[i : i + LANES, :] + v
            top = jnp.max(s, axis=1, keepdims=True)
            p = jnp.exp2(s - top)
            total = jnp.sum(p, axis=1, keepdims=True)
            if last:
                plan[i : i + LANES, :] = p.astype(jnp.bfloat16)
                top_col[i : i + LANES, :] = top
            box[col, :, i : i + LANES] = to_lanes(top + jnp.log(total) * LOG2E, mask)

    def row_finish(box):
        u = -merge(box, float(n_col * cols))
        u_line[...] = u
        for i in range(0, rows, LANES):
            u_col[i : i + LANES, :] = to_sublanes(u[:, i : i + LANES], mask)

    def col_local(box):
        u = u_col[...]
        for j in range(0, cols, LANES):
            s = scores[:, j : j + LANES] + u
            top = jnp.max(s, axis=0, keepdims=True)
            total = jnp.sum(jnp.exp2(s - top), axis=0, keepdims=True)
            box[row, :, j : j + LANES] = top + jnp.log(total) * LOG2E

    for step in range(ITERS):
        box = row_box.at[step]
        row_local(box, False)
        share(box, col, row_peer)
        settle(box)
        row_finish(box)
        box = col_box.at[step]
        col_local(box)
        share(box, row, col_peer)
        settle(box)
        v_line[...] = -merge(box, float(n_row * rows))
    box = row_box.at[ITERS]
    row_local(box, True)
    share(box, col, row_peer)
    settle(box)
    row_finish(box)
    for i in range(0, rows, LANES):
        s = to_lanes(jnp.sum(noise_sq[i : i + LANES, :], axis=1, keepdims=True), mask)
        row_ref[:, i : i + LANES] = u_line[:, i : i + LANES] * (EPS / LOG2E) + s / width
    col_ref[...] = col_ref[...] / width + v_line[...] * (EPS / LOG2E)
    u_col[...] = jnp.exp2(u_col[...] + top_col[...]) / float(n_col * cols)

    def product(k):
        r = jnp.dot(plan[...], data_all[k], preferred_element_type=jnp.float32)
        return r * u_col[...]

    order = [(o, z_) for o in (y_far, y_next, y_prev, y) for z_ in (1 - zh, zh)]
    give = []
    for t, (o, z_) in enumerate(order):
        to_twin[t] = product(col_of(o, z_, 1 - core)).astype(jnp.bfloat16)
        give.append(send(to_twin.at[t], from_twin.at[t], twin))
    for t, (o, z_) in enumerate(order):
        r = product(col_of(o, z_, core))
        give[t].wait_recv()
        own[t] = r + from_twin[t].astype(jnp.float32)
    lo, hi = pl.ds(0, half_n), pl.ds(half_n, half_n)
    up, down = (row, col_of(y_next, zh, core)), (row, col_of(y_prev, zh, core))
    relays = []
    for t in (0, 1):
        relay_out[t] = own[t].astype(jnp.bfloat16)
        relays.append(
            (
                send(relay_out.at[t, lo], relay_in.at[t, lo], up),
                send(relay_out.at[t, hi], relay_in.at[t, hi], down),
            )
        )
    pairs = []
    for t in (0, 1):
        relays[t][0].wait_recv()
        pair_out[0, t, lo] = (own[2 + t, lo] + relay_in[t, lo].astype(jnp.float32)).astype(jnp.bfloat16)
        pair_out[0, t, hi] = own[2 + t, hi].astype(jnp.bfloat16)
        a = send(pair_out.at[0, t], pair_in.at[0, t], up)
        relays[t][1].wait_recv()
        pair_out[1, t, lo] = own[4 + t, lo].astype(jnp.bfloat16)
        pair_out[1, t, hi] = (own[4 + t, hi] + relay_in[t, hi].astype(jnp.float32)).astype(jnp.bfloat16)
        b = send(pair_out.at[1, t], pair_in.at[1, t], down)
        pairs.append((a, b))

    def total(t):
        pairs[t][0].wait_recv()
        pairs[t][1].wait_recv()
        return own[6 + t] + pair_in[0, t].astype(jnp.float32) + pair_in[1, t].astype(jnp.float32)

    z_out[...] = total(0).astype(jnp.bfloat16)
    over = send(z_out, z_in, partner)
    mine = total(1)
    over.wait_recv()
    targets_ref[...] = (mine + z_in[...].astype(jnp.float32)).astype(jnp.bfloat16)

    for copy in started:
        copy.wait_send()


COPIES = 80


def body(noise, data):
    rows, part = noise.shape
    cols = data.shape[0]
    width = part * 16
    vmem = pl.BlockSpec(memory_space=pltpu.VMEM)
    bf16, f32 = jnp.bfloat16, jnp.float32
    flops = 2 * 2 * rows * cols * width
    targets, row_potential, col_potential = pl.pallas_call(
        functools.partial(kernel, width),
        out_shape=(
            jax.ShapeDtypeStruct((rows, part), bf16),
            jax.ShapeDtypeStruct((1, rows), f32),
            jax.ShapeDtypeStruct((1, cols), f32),
        ),
        in_specs=[vmem] * 2,
        out_specs=[vmem] * 3,
        scratch_shapes=[
            pltpu.VMEM((16, rows, part), bf16),
            pltpu.VMEM((16, cols, part), bf16),
            pltpu.VMEM((rows, cols), f32),
            pltpu.VMEM((rows, cols), bf16),
            pltpu.VMEM((rows, 1), f32),
            pltpu.VMEM((1, rows), f32),
            pltpu.VMEM((1, cols), f32),
            pltpu.VMEM((rows, 1), f32),
            pltpu.VMEM((rows, LANES), f32),
            pltpu.VMEM((cols, LANES), f32),
            pltpu.VMEM((ITERS + 1, 16, 1, rows), f32),
            pltpu.VMEM((ITERS, 16, 1, cols), f32),
            pltpu.VMEM((8, rows, part), bf16),
            pltpu.VMEM((8, rows, part), bf16),
            pltpu.VMEM((8, rows, part), f32),
            pltpu.VMEM((2, rows, part), bf16),
            pltpu.VMEM((2, rows, part), bf16),
            pltpu.VMEM((2, 2, rows, part), bf16),
            pltpu.VMEM((2, 2, rows, part), bf16),
            pltpu.VMEM((rows, part), bf16),
            pltpu.VMEM((rows, part), bf16),
            pltpu.SemaphoreType.DMA((COPIES,)),
            pltpu.SemaphoreType.DMA((COPIES,)),
            pltpu.SemaphoreType.DMA((2 * ITERS + 1,)),
            pltpu.SemaphoreType.DMA((2 * ITERS + 1,)),
        ],
        compiler_params=pltpu.CompilerParams(
            collective_id=0,
            has_side_effects=True,
            vmem_limit_bytes=48 * 1024 * 1024,
        ),
        cost_estimate=pl.CostEstimate(
            flops=flops, bytes_accessed=2 * (rows + cols) * part * 2, transcendentals=8 * rows * cols
        ),
    )(noise, data)
    return targets, row_potential.reshape(rows), col_potential.reshape(cols)


def solution(mesh):
    return jax.shard_map(
        body,
        mesh=mesh,
        in_specs=(P("row", "col"), P("col", "row")),
        out_specs=(P("row", "col"), P("row"), P("col")),
        check_vma=False,
    )
```

```python
import functools
import math

import jax
import jax.numpy as jnp
from jax import lax
from jax.experimental import pallas as pl
from jax.experimental.pallas import tpu as pltpu
from jax.sharding import PartitionSpec as P

ITERS = 3
EPS = 0.01
LOG2E = math.log2(math.e)
MESH = pl.DeviceIdType.MESH
NT = (((1,), (1,)), ((), ()))
LANES = 128


def eye():
    r = lax.broadcasted_iota(jnp.int32, (LANES, LANES), 0)
    c = lax.broadcasted_iota(jnp.int32, (LANES, LANES), 1)
    return r == c


def to_lanes(column, mask):
    return jnp.sum(jnp.where(mask, column, 0.0), axis=0, keepdims=True)


def to_sublanes(line, mask):
    return jnp.sum(jnp.where(mask, line, 0.0), axis=1, keepdims=True)


def kernel(
    width,
    noise_ref,
    data_ref,
    targets_ref,
    row_ref,
    col_ref,
    noise_all,
    data_all,
    scores,
    plan,
    u_col,
    u_line,
    v_line,
    noise_sq,
    data_sq,
    row_box,
    col_box,
    twin_line,
    to_twin,
    from_twin,
    own,
    relay_out,
    relay_in,
    direct_out,
    direct_in,
    summed_out,
    summed_in,
    z_out,
    z_in,
    weight,
    send_sem,
    recv_sem,
    box_send,
    box_recv,
):
    rows, part = noise_ref.shape
    cols = data_ref.shape[0]
    n_row, n_col = 16, 16
    row, col = lax.axis_index("row"), lax.axis_index("col")
    x, zl = row // 4, row % 4
    y, zh, core = col // 4, (col // 2) % 2, col % 2
    mask = eye()
    started = []

    def row_of(x_, zl_):
        return x_ * 4 + zl_

    def col_of(y_, zh_, core_):
        return (y_ * 2 + zh_) * 2 + core_

    def send(src, dst, to, lands=None, where=None, size=None):
        n = len(started)
        started.append((src if size is None else size, n, where))
        copy = pltpu.make_async_remote_copy(
            src_ref=src,
            dst_ref=dst,
            send_sem=send_sem.at[n],
            recv_sem=recv_sem.at[n if lands is None else lands],
            device_id=to,
            device_id_type=MESH,
        )
        copy.start()
        return copy

    x_next, x_prev = lax.rem(x + 1, 4), lax.rem(x + 3, 4)
    y_next, y_prev = lax.rem(y + 1, 4), lax.rem(y + 3, 4)
    x_far, y_far = lax.rem(x + 2, 4), lax.rem(y + 2, 4)
    aside, across = zl + 1 - 2 * lax.rem(zl, 2), 3 - zl
    source = (zl, aside, 2 - zl // 2, 3 - 3 * (zl // 2))
    middle = (zl == 1) | (zl == 2)
    half_d, half_n = cols // 2, rows // 2
    halves_d = (pl.ds(0, half_d), pl.ds(half_d, half_d))
    halves_n = (pl.ds(0, half_n), pl.ds(half_n, half_n))
    twin = (row, col_of(y, zh, 1 - core))
    partner = (row, col_of(y, 1 - zh, core))
    right, left = (row_of(x_next, zl), col), (row_of(x_prev, zl), col)
    up, down = (row, col_of(y_next, zh, core)), (row, col_of(y_prev, zh, core))
    z_aside, z_across = (row_of(x, aside), col), (row_of(x, across), col)

    barrier = pltpu.get_barrier_semaphore()
    greeted = (twin, right, left, up, down, z_aside, z_across, partner)
    for to in greeted:
        pl.semaphore_signal(barrier, inc=1, device_id=to, device_id_type=MESH)
    noise_all[col] = noise_ref[...]
    data_all[row] = data_ref[...]
    scores[...] = jnp.zeros_like(scores)
    noise_sq[...] = jnp.zeros_like(noise_sq)
    data_sq[...] = jnp.zeros_like(data_sq)
    pl.semaphore_wait(barrier, len(greeted))

    def accumulate(k):
        a, b = noise_all[k], data_all[k]
        scores[...] += lax.dot_general(a, b, NT, preferred_element_type=jnp.float32)
        a, b = a.astype(jnp.float32), b.astype(jnp.float32)
        a, b = a * a, b * b
        noise_sq[...] += a[:, :LANES] + a[:, LANES:]
        data_sq[...] += b[:, :LANES] + b[:, LANES:]

    def gathers():
        class Ring:
            def __init__(self, array, halves, slot_of, after, before):
                self.array, self.halves, self.slot_of = array, halves, slot_of
                self.after, self.before = after, before

            def part(self, place, h):
                return self.array.at[self.slot_of(place), self.halves[h]]

            def start(self, h):
                block = self.part(0, h)
                ways = (self.after, self.before) if h == 0 else (self.before, self.after)
                first, second = (send(block, block, to) for to in ways)
                if h == 0:
                    self.lo_after, self.lo_before = first, second
                else:
                    self.hi_before, self.hi_after = first, second

            def pass_on(self):
                self.lo_after.wait_recv()
                block = self.part(3, 0)
                self.far_lo = send(block, block, self.after)
                self.hi_before.wait_recv()
                block = self.part(1, 1)
                self.far_hi = send(block, block, self.before)

            def near(self):
                self.hi_after.wait_recv()
                self.lo_before.wait_recv()

            def far(self):
                self.far_lo.wait_recv()
                self.far_hi.wait_recv()

        def data_slot(k):
            return lambda i: row_of(lax.rem(x + i, 4), source[k])

        def noise_slot(z_):
            return lambda i: col_of(lax.rem(y + i, 4), z_, core)

        data_rings = [Ring(data_all, halves_d, data_slot(k), right, left) for k in range(4)]
        noise_rings = [Ring(noise_all, halves_n, noise_slot(z_), up, down) for z_ in (zh, 1 - zh)]
        twins = []

        def to_the_twin(ring, i):
            block = noise_all.at[ring.slot_of(i)]
            twins.append(send(block, block, twin))

        def z_part(k, h):
            return data_all.at[row_of(x, source[k]), halves_d[h]]

        sizes = [z_part(0, h) for h in (0, 1)]

        def z_send(k, h, to, where=None):
            block = z_part(k, h)
            send(block, block, to, LINE + source[k] * 2 + h, where, sizes[h])

        def z_arrive(k, h):
            block = z_part(k, h)
            pltpu.make_async_copy(block, block, recv_sem.at[LINE + source[k] * 2 + h]).wait()

            @pl.when(middle)
            def _():
                z_send(k, h, z_across if k == 1 else z_aside, middle)

            data_rings[k].start(h)

        crossing = []
        for h in (0, 1):
            block = noise_all.at[col, halves_n[h]]
            crossing.append(send(block, block, partner))
            z_send(0, h, z_aside)
        @pl.when(middle)
        def _():
            for h in (0, 1):
                z_send(0, h, z_across, middle)
        for h in (0, 1):
            data_rings[0].start(h)
        for h in (0, 1):
            noise_rings[0].start(h)
        to_the_twin(noise_rings[0], 0)

        z_arrive(1, 0)
        data_rings[0].pass_on()
        noise_rings[0].pass_on()
        z_arrive(1, 1)
        noise_rings[0].near()
        to_the_twin(noise_rings[0], 3)
        to_the_twin(noise_rings[0], 1)
        z_arrive(2, 0)
        z_arrive(2, 1)
        data_rings[1].pass_on()
        noise_rings[0].far()
        to_the_twin(noise_rings[0], 2)
        for h in (0, 1):
            crossing[h].wait_recv()
            noise_rings[1].start(h)
        to_the_twin(noise_rings[1], 0)
        z_arrive(3, 0)
        z_arrive(3, 1)
        data_rings[2].pass_on()
        noise_rings[1].pass_on()
        noise_rings[1].near()
        to_the_twin(noise_rings[1], 3)
        to_the_twin(noise_rings[1], 1)
        noise_rings[1].far()
        to_the_twin(noise_rings[1], 2)
        for t in twins:
            t.wait_recv()

        def add_group(k):
            def one(i, carry):
                accumulate(data_slot(k)(i))
                return carry

            lax.fori_loop(0, 4, one, 0)

        for k in (0, 1):
            data_rings[k].near()
            data_rings[k].far()
            add_group(k)
        data_rings[3].pass_on()
        data_rings[2].near()
        data_rings[2].far()
        add_group(2)
        accumulate(data_slot(3)(0))
        data_rings[3].near()
        accumulate(data_slot(3)(1))
        accumulate(data_slot(3)(3))
        data_rings[3].far()
        accumulate(data_slot(3)(2))

        unit = LOG2E / (EPS * width)
        for i in range(0, rows, LANES):
            scores[i : i + LANES, :] = scores[i : i + LANES, :] * (2.0 * unit)
        for j in range(0, cols, LANES):
            s = to_lanes(jnp.sum(data_sq[j : j + LANES, :], axis=1, keepdims=True), mask)
            col_ref[:, j : j + LANES] = s
            v_line[:, j : j + LANES] = s * -unit

    def updates():
        def share(box, mine, peer_of):
            def one(d, carry):
                pltpu.make_async_remote_copy(
                    src_ref=box.at[mine],
                    dst_ref=box.at[mine],
                    send_sem=box_send.at[shared[0]],
                    recv_sem=box_recv.at[shared[0]],
                    device_id=peer_of(d),
                    device_id_type=MESH,
                ).start()
                return carry

            lax.fori_loop(1, 16, one, 0)

        def settle(box):
            n = shared[0]
            shared[0] += 1
            many = box.at[pl.ds(0, 15)]
            pltpu.make_async_copy(many, many, box_recv.at[n]).wait()
            pltpu.make_async_copy(many, many, box_send.at[n]).wait()

        shared = [0]

        def row_peer(d):
            return (row, lax.rem(col + d, n_col))

        def col_peer(d):
            return (lax.rem(row + d, n_row), col)

        def merge(box, count):
            lines = box[...]
            top = jnp.max(lines, axis=0)
            total = jnp.sum(jnp.exp2(lines - top[None]), axis=0)
            return top + jnp.log(total / count) * LOG2E

        def row_local(box, last):
            v = v_line[...]
            for i in range(0, rows, LANES):
                s = scores[i : i + LANES, :] + v
                top = jnp.max(s, axis=1, keepdims=True)
                p = jnp.exp2(s - top)
                total = jnp.sum(p, axis=1, keepdims=True)
                if last:
                    plan[i : i + LANES, :] = (p * (1.0 / total)).astype(jnp.bfloat16)
                box[col, :, i : i + LANES] = to_lanes(top + jnp.log(total) * LOG2E, mask)

        def row_finish(box):
            u = -merge(box, float(n_col * cols))
            u_line[...] = u
            for i in range(0, rows, LANES):
                u_col[i : i + LANES, :] = to_sublanes(u[:, i : i + LANES], mask)

        def col_local(box):
            u = u_col[...]
            for j in range(0, cols, LANES):
                s = scores[:, j : j + LANES] + u
                top = jnp.max(s, axis=0, keepdims=True)
                total = jnp.sum(jnp.exp2(s - top), axis=0, keepdims=True)
                box[row, :, j : j + LANES] = top + jnp.log(total) * LOG2E

        for step in range(ITERS):
            box = row_box.at[step]
            row_local(box, False)
            share(box, col, row_peer)
            settle(box)
            row_finish(box)
            box = col_box.at[step]
            col_local(box)
            share(box, row, col_peer)
            settle(box)
            v_line[...] = -merge(box, float(n_row * rows))
        box = row_box.at[ITERS]
        row_local(box, True)
        of_twin = send(box.at[col], twin_line, twin)
        share(box, col, row_peer)

        def product(k):
            return jnp.dot(plan[...], data_all[k], preferred_element_type=jnp.float32)

        def spread(line):
            return [to_sublanes(line[:, i : i + LANES], mask) for i in range(0, rows, LANES)]

        order = [(o, z_) for z_ in (1 - zh, zh) for o in (y_far, y_next, y_prev, y)]
        give = []
        for t, (o, z_) in enumerate(order):
            to_twin[t] = product(col_of(o, z_, 1 - core)).astype(jnp.bfloat16)
            give.append(send(to_twin.at[t], from_twin.at[t], twin))
        of_twin.wait_recv()
        mine, other = box[col], twin_line[...]
        top = jnp.maximum(mine, other)
        a, b = jnp.exp2(mine - top), jnp.exp2(other - top)
        weight[0] = jnp.concatenate(spread(a / (a + b)), axis=0)
        weight[1] = jnp.concatenate(spread(b / (a + b)), axis=0)

        def own_sum(t):
            o, z_ = order[t]
            r = product(col_of(o, z_, core)) * weight[0]
            give[t].wait_recv()
            own[t] = r + from_twin[t].astype(jnp.float32) * weight[1]

        lo, hi = halves_n
        sent = {}

        def relay(g):
            own_sum(4 * g)
            relay_out[g] = own[4 * g].astype(jnp.bfloat16)
            sent[g, "lo"] = send(relay_out.at[g, lo], relay_in.at[g, lo], up)
            sent[g, "hi"] = send(relay_out.at[g, hi], relay_in.at[g, hi], down)

        def direct(g):
            direct_out[g, hi] = own[4 * g + 1, hi].astype(jnp.bfloat16)
            sent[g, "dhi"] = send(direct_out.at[g, hi], direct_in.at[g, hi], up)
            direct_out[g, lo] = own[4 * g + 2, lo].astype(jnp.bfloat16)
            sent[g, "dlo"] = send(direct_out.at[g, lo], direct_in.at[g, lo], down)

        def summed(g):
            sent[g, "lo"].wait_recv()
            summed_out[g, lo] = (
                own[4 * g + 1, lo] * weight[2, lo] + relay_in[g, lo].astype(jnp.float32) * weight[3, lo]
            ).astype(jnp.bfloat16)
            sent[g, "slo"] = send(summed_out.at[g, lo], summed_in.at[g, lo], up)
            sent[g, "hi"].wait_recv()
            summed_out[g, hi] = (
                own[4 * g + 2, hi] * weight[2, hi] + relay_in[g, hi].astype(jnp.float32) * weight[4, hi]
            ).astype(jnp.bfloat16)
            sent[g, "shi"] = send(summed_out.at[g, hi], summed_in.at[g, hi], down)

        def total(g, half, name, sender):
            sent[g, "d" + name].wait_recv()
            r = own[4 * g + 3, half] * weight[2, half] + direct_in[g, half].astype(jnp.float32) * weight[sender, half]
            sent[g, "s" + name].wait_recv()
            return r + summed_in[g, half].astype(jnp.float32)

        relay(0)
        own_sum(1)
        own_sum(2)
        direct(0)
        relay(1)
        own_sum(3)
        own_sum(5)
        own_sum(6)
        settle(box)
        row_finish(box)
        u = u_line[...]
        scale = 1.0 / float(n_col * cols)
        for n, o in ((2, y), (3, y_prev), (4, y_next)):
            share_of = jnp.exp2(box[col_of(o, zh, 0)] + u) + jnp.exp2(box[col_of(o, zh, 1)] + u)
            weight[n] = jnp.concatenate(spread(share_of * (scale)), axis=0)
        summed(0)
        direct(1)
        own_sum(7)
        cross = []
        for half, name, sender in ((lo, "lo", 4), (hi, "hi", 3)):
            z_out[half] = total(0, half, name, sender).astype(jnp.bfloat16)
            cross.append(send(z_out.at[half], z_in.at[half], partner))
        summed(1)
        for i in range(0, rows, LANES):
            s = to_lanes(jnp.sum(noise_sq[i : i + LANES, :], axis=1, keepdims=True), mask)
            row_ref[:, i : i + LANES] = u_line[:, i : i + LANES] * (EPS / LOG2E) + s / width
        col_ref[...] = col_ref[...] / width + v_line[...] * (EPS / LOG2E)
        for half, name, sender, c in ((lo, "lo", 4, cross[0]), (hi, "hi", 3, cross[1])):
            r = total(1, half, name, sender)
            c.wait_recv()
            targets_ref[half] = (r + z_in[half].astype(jnp.float32)).astype(jnp.bfloat16)

    gathers()
    updates()
    for ref, n, where in started:
        wait = pltpu.make_async_copy(ref, ref, send_sem.at[n]).wait
        if where is None:
            wait()
        else:
            pl.when(where)(wait)


LINE = 120
COPIES = LINE + 8


def body(noise, data):
    rows, part = noise.shape
    cols = data.shape[0]
    width = part * 16
    vmem = pl.BlockSpec(memory_space=pltpu.VMEM)
    bf16, f32 = jnp.bfloat16, jnp.float32
    flops = 2 * 2 * rows * cols * width
    targets, row_potential, col_potential = pl.pallas_call(
        functools.partial(kernel, width),
        out_shape=(
            jax.ShapeDtypeStruct((rows, part), bf16),
            jax.ShapeDtypeStruct((1, rows), f32),
            jax.ShapeDtypeStruct((1, cols), f32),
        ),
        in_specs=[vmem] * 2,
        out_specs=[vmem] * 3,
        scratch_shapes=[
            pltpu.VMEM((16, rows, part), bf16),
            pltpu.VMEM((16, cols, part), bf16),
            pltpu.VMEM((rows, cols), f32),
            pltpu.VMEM((rows, cols), bf16),
            pltpu.VMEM((rows, 1), f32),
            pltpu.VMEM((1, rows), f32),
            pltpu.VMEM((1, cols), f32),
            pltpu.VMEM((rows, LANES), f32),
            pltpu.VMEM((cols, LANES), f32),
            pltpu.VMEM((ITERS + 1, 16, 1, rows), f32),
            pltpu.VMEM((ITERS, 16, 1, cols), f32),
            pltpu.VMEM((1, rows), f32),
            pltpu.VMEM((8, rows, part), bf16),
            pltpu.VMEM((8, rows, part), bf16),
            pltpu.VMEM((8, rows, part), f32),
            *[pltpu.VMEM((2, rows, part), bf16)] * 6,
            *[pltpu.VMEM((rows, part), bf16)] * 2,
            pltpu.VMEM((5, rows, 1), f32),
            pltpu.SemaphoreType.DMA((COPIES,)),
            pltpu.SemaphoreType.DMA((COPIES,)),
            pltpu.SemaphoreType.DMA((2 * ITERS + 1,)),
            pltpu.SemaphoreType.DMA((2 * ITERS + 1,)),
        ],
        compiler_params=pltpu.CompilerParams(
            collective_id=0,
            has_side_effects=True,
            vmem_limit_bytes=48 * 1024 * 1024,
        ),
        cost_estimate=pl.CostEstimate(
            flops=flops, bytes_accessed=2 * (rows + cols) * part * 2, transcendentals=8 * rows * cols
        ),
    )(noise, data)
    return targets, row_potential.reshape(rows), col_potential.reshape(cols)


def solution(mesh):
    return jax.shard_map(
        body,
        mesh=mesh,
        in_specs=(P("row", "col"), P("col", "row")),
        out_specs=(P("row", "col"), P("row"), P("col")),
        check_vma=False,
    )
```

```python
import functools
import math

import jax
import jax.numpy as jnp
from jax import lax
from jax.experimental import pallas as pl
from jax.experimental.pallas import tpu as pltpu
from jax.sharding import PartitionSpec as P

ITERS = 3
EPS = 0.01
LOG2E = math.log2(math.e)
MESH = pl.DeviceIdType.MESH
NT = (((1,), (1,)), ((), ()))
LANES = 128


def eye():
    r = lax.broadcasted_iota(jnp.int32, (LANES, LANES), 0)
    c = lax.broadcasted_iota(jnp.int32, (LANES, LANES), 1)
    return r == c


def to_lanes(column, mask):
    return jnp.sum(jnp.where(mask, column, 0.0), axis=0, keepdims=True)


def to_sublanes(line, mask):
    return jnp.sum(jnp.where(mask, line, 0.0), axis=1, keepdims=True)


def kernel(
    width,
    noise_ref,
    data_ref,
    targets_ref,
    row_ref,
    col_ref,
    noise_all,
    data_all,
    scores,
    plan,
    u_col,
    v_line,
    noise_sq,
    data_sq,
    row_box,
    col_box,
    twin_line,
    to_twin,
    from_twin,
    own,
    first_out,
    first_in,
    relay_out,
    relay_in,
    direct_out,
    direct_in,
    summed_out,
    summed_in,
    z_out,
    z_in,
    weight,
    send_sem,
    recv_sem,
    box_send,
    box_recv,
):
    rows, part = noise_ref.shape
    cols = data_ref.shape[0]
    n_row, n_col = 16, 16
    row, col = lax.axis_index("row"), lax.axis_index("col")
    x, zl = row // 4, row % 4
    y, zh, core = col // 4, (col // 2) % 2, col % 2
    mask = eye()
    started = []

    def row_of(x_, zl_):
        return x_ * 4 + zl_

    def col_of(y_, zh_, core_):
        return (y_ * 2 + zh_) * 2 + core_

    def send(src, dst, to, lands=None, where=None, size=None):
        n = len(started)
        started.append((src if size is None else size, n, where))
        copy = pltpu.make_async_remote_copy(
            src_ref=src,
            dst_ref=dst,
            send_sem=send_sem.at[n],
            recv_sem=recv_sem.at[n if lands is None else lands],
            device_id=to,
            device_id_type=MESH,
        )
        copy.start()
        return copy

    x_next, x_prev = lax.rem(x + 1, 4), lax.rem(x + 3, 4)
    y_next, y_prev = lax.rem(y + 1, 4), lax.rem(y + 3, 4)
    x_far, y_far = lax.rem(x + 2, 4), lax.rem(y + 2, 4)
    aside, across = zl + 1 - 2 * lax.rem(zl, 2), 3 - zl
    source = (zl, aside, 2 - zl // 2, 3 - 3 * (zl // 2))
    middle = (zl == 1) | (zl == 2)
    twin = (row, col_of(y, zh, 1 - core))
    partner = (row, col_of(y, 1 - zh, core))
    right, left = (row_of(x_next, zl), col), (row_of(x_prev, zl), col)
    up, down = (row, col_of(y_next, zh, core)), (row, col_of(y_prev, zh, core))
    z_aside, z_across = (row_of(x, aside), col), (row_of(x, across), col)

    barrier = pltpu.get_barrier_semaphore()
    greeted = (twin, right, left, up, down, z_aside, z_across, partner)
    for to in greeted:
        pl.semaphore_signal(barrier, inc=1, device_id=to, device_id_type=MESH)
    noise_all[col] = noise_ref[...]
    data_all[row] = data_ref[...]
    scores[...] = jnp.zeros_like(scores)
    noise_sq[...] = jnp.zeros_like(noise_sq)
    data_sq[...] = jnp.zeros_like(data_sq)
    pl.semaphore_wait(barrier, len(greeted))

    def accumulate(k):
        a, b = noise_all[k], data_all[k]
        scores[...] += lax.dot_general(a, b, NT, preferred_element_type=jnp.float32)
        a, b = a.astype(jnp.float32), b.astype(jnp.float32)
        a, b = a * a, b * b
        noise_sq[...] += a[:, :LANES] + a[:, LANES:]
        data_sq[...] += b[:, :LANES] + b[:, LANES:]

    def gathers():
        class Ring:
            def __init__(self, array, step, slot_of, after, before):
                self.array, self.step, self.slot_of = array, step, slot_of
                self.after, self.before = after, before
                self.sent = {}

            def part(self, place, p):
                return self.array.at[self.slot_of(place), pl.ds(p * self.step, self.step)]

            def start(self, p):
                block = self.part(0, p)
                ways = (self.after, self.before) if p < PARTS // 2 else (self.before, self.after)
                self.sent[p] = [send(block, block, to) for to in ways]

            def pass_on(self, p):
                self.sent[p][0].wait_recv()
                place, to = (3, self.after) if p < PARTS // 2 else (1, self.before)
                block = self.part(place, p)
                self.sent[p].append(send(block, block, to))

            def near(self):
                for p in ORDER:
                    self.sent[p][1].wait_recv()

            def far(self):
                for p in ORDER:
                    self.sent[p][2].wait_recv()

        def data_slot(k):
            return lambda i: row_of(lax.rem(x + i, 4), source[k])

        def noise_slot(z_):
            return lambda i: col_of(lax.rem(y + i, 4), z_, core)

        d = [Ring(data_all, cols // PARTS, data_slot(k), right, left) for k in range(4)]
        n = [Ring(noise_all, rows // PARTS, noise_slot(z_), up, down) for z_ in (zh, 1 - zh)]
        twins, crossing = [], {}

        def to_the_twin(ring, *places):
            for i in places:
                block = noise_all.at[ring.slot_of(i)]
                twins.append(send(block, block, twin))

        def z_part(k, p):
            return data_all.at[row_of(x, source[k]), pl.ds(p * (cols // PARTS), cols // PARTS)]

        size = z_part(0, 0)

        def z_send(k, p, to, where=None):
            block = z_part(k, p)
            send(block, block, to, LINE + source[k] * PARTS + p, where, size)

        def z_arrive(k, p):
            block = z_part(k, p)
            pltpu.make_async_copy(block, block, recv_sem.at[LINE + source[k] * PARTS + p]).wait()

            @pl.when(middle)
            def _():
                z_send(k, p, z_across if k == 1 else z_aside, middle)

            d[k].start(p)

        def cross(p):
            block = n[0].part(0, p)
            crossing[p] = send(block, block, partner)

        def cross_arrive(p):
            crossing[p].wait_recv()
            n[1].start(p)

        for p in ORDER:
            z_send(0, p, z_aside)
            d[0].start(p)

        @pl.when(middle)
        def _():
            for p in ORDER:
                z_send(0, p, z_across, middle)

        for p in ORDER:
            cross(p)
        for p in ORDER:
            n[0].start(p)
        to_the_twin(n[0], 0)
        for p in ORDER:
            z_arrive(1, p)
            d[0].pass_on(p)
        for p in ORDER:
            n[0].pass_on(p)
        for p in ORDER:
            z_arrive(2, p)
            d[1].pass_on(p)
        n[0].near()
        to_the_twin(n[0], 3, 1)
        n[0].far()
        to_the_twin(n[0], 2)
        for p in ORDER:
            cross_arrive(p)
        for p in ORDER:
            z_arrive(3, p)
        to_the_twin(n[1], 0)
        for p in ORDER:
            d[2].pass_on(p)
        for p in ORDER:
            n[1].pass_on(p)
        n[1].near()
        to_the_twin(n[1], 3, 1)
        n[1].far()
        to_the_twin(n[1], 2)
        for p in ORDER:
            d[3].pass_on(p)
        for t in twins:
            t.wait_recv()

        def add_group(k):
            def one(i, carry):
                accumulate(data_slot(k)(i))
                return carry

            lax.fori_loop(0, 4, one, 0)

        for k in (0, 1, 2):
            d[k].near()
            d[k].far()
            add_group(k)
        accumulate(data_slot(3)(0))
        d[3].near()
        accumulate(data_slot(3)(1))
        accumulate(data_slot(3)(3))
        d[3].far()
        accumulate(data_slot(3)(2))

        unit = LOG2E / (EPS * width)
        for i in range(0, rows, LANES):
            scores[i : i + LANES, :] = scores[i : i + LANES, :] * (2.0 * unit)
        for j in range(0, cols, LANES):
            s = to_lanes(jnp.sum(data_sq[j : j + LANES, :], axis=1, keepdims=True), mask)
            col_ref[:, j : j + LANES] = s
            v_line[:, j : j + LANES] = s * -unit

    def updates():
        def share(box, mine, peer_of):
            def one(d, carry):
                pltpu.make_async_remote_copy(
                    src_ref=box.at[mine],
                    dst_ref=box.at[mine],
                    send_sem=box_send.at[shared[0]],
                    recv_sem=box_recv.at[shared[0]],
                    device_id=peer_of(d),
                    device_id_type=MESH,
                ).start()
                return carry

            lax.fori_loop(1, 16, one, 0)

        def settle(box):
            n = shared[0]
            shared[0] += 1
            many = box.at[pl.ds(0, 15)]
            pltpu.make_async_copy(many, many, box_recv.at[n]).wait()
            pltpu.make_async_copy(many, many, box_send.at[n]).wait()

        shared = [0]

        def row_peer(d):
            return (row, lax.rem(col + d, n_col))

        def col_peer(d):
            return (lax.rem(row + d, n_row), col)

        def merge(box, count):
            lines = box[...]
            top = jnp.max(lines, axis=0)
            total = jnp.sum(jnp.exp2(lines - top[None]), axis=0)
            return top + jnp.log(total / count) * LOG2E

        def row_local(box, last):
            v = v_line[...]
            for i in range(0, rows, LANES):
                s = scores[i : i + LANES, :] + v
                top = jnp.max(s, axis=1, keepdims=True)
                p = jnp.exp2(s - top)
                total = jnp.sum(p, axis=1, keepdims=True)
                if last:
                    plan[i : i + LANES, :] = (p * (1.0 / total)).astype(jnp.bfloat16)
                box[col, :, i : i + LANES] = to_lanes(top + jnp.log(total) * LOG2E, mask)

        def row_finish(box):
            u = -merge(box, float(n_col * cols))
            for i in range(0, rows, LANES):
                u_col[i : i + LANES, :] = to_sublanes(u[:, i : i + LANES], mask)

        def col_local(box):
            u = u_col[...]
            for j in range(0, cols, LANES):
                s = scores[:, j : j + LANES] + u
                top = jnp.max(s, axis=0, keepdims=True)
                total = jnp.sum(jnp.exp2(s - top), axis=0, keepdims=True)
                box[row, :, j : j + LANES] = top + jnp.log(total) * LOG2E

        for step in range(ITERS):
            box = row_box.at[step]
            row_local(box, False)
            share(box, col, row_peer)
            settle(box)
            row_finish(box)
            box = col_box.at[step]
            col_local(box)
            share(box, row, col_peer)
            settle(box)
            v_line[...] = -merge(box, float(n_row * rows))
        box = row_box.at[ITERS]
        row_local(box, True)
        of_twin = send(box.at[col], twin_line, twin)
        share(box, col, row_peer)

        def product(k):
            return jnp.dot(plan[...], data_all[k], preferred_element_type=jnp.float32)

        def spread(line):
            return [to_sublanes(line[:, i : i + LANES], mask) for i in range(0, rows, LANES)]

        order = [(o, z_) for z_ in (1 - zh, zh) for o in (y_far, y_next, y_prev, y)]
        give = {}

        def twin_sum(t):
            o, z_ = order[t]
            to_twin[t] = product(col_of(o, z_, 1 - core)).astype(jnp.bfloat16)
            give[t] = send(to_twin.at[t], from_twin.at[t], twin)

        def own_sum(t):
            o, z_ = order[t]
            r = product(col_of(o, z_, core)) * weight[0]
            give[t].wait_recv()
            own[t] = r + from_twin[t].astype(jnp.float32) * weight[1]

        step = rows // PARTS
        parts = [pl.ds(p * step, step) for p in range(PARTS)]
        low = [p < PARTS // 2 for p in range(PARTS)]
        relayed, directly, further, over, straight = {}, {}, {}, {}, {}

        def first():
            for p in ORDER:
                for i, there in enumerate(((row, col_of(y_far, zh, core)), up, down)):
                    first_out[i, parts[p]] = own[i, parts[p]].astype(jnp.bfloat16)
                    straight[i, p] = send(first_out.at[i, parts[p]], first_in.at[i, parts[p]], there)

        def first_total(p):
            part = parts[p]
            r = own[3, part] * weight[2, part]
            for i, sender in ((0, 5), (1, 3), (2, 4)):
                straight[i, p].wait_recv()
                r += first_in[i, part].astype(jnp.float32) * weight[sender, part]
            return r

        def relay(g):
            relay_out[g] = own[4 * g].astype(jnp.bfloat16)
            for p in ORDER:
                there = up if low[p] else down
                relayed[g, p] = send(relay_out.at[g, parts[p]], relay_in.at[g, parts[p]], there)

        def direct(g):
            for p in ORDER:
                t, there = (4 * g + 2, down) if low[p] else (4 * g + 1, up)
                direct_out[g, parts[p]] = own[t, parts[p]].astype(jnp.bfloat16)
                directly[g, p] = send(direct_out.at[g, parts[p]], direct_in.at[g, parts[p]], there)

        def summed(g):
            for p in ORDER:
                t, there, sender = (4 * g + 1, up, 3) if low[p] else (4 * g + 2, down, 4)
                relayed[g, p].wait_recv()
                part = parts[p]
                r = own[t, part] * weight[2, part] + relay_in[g, part].astype(jnp.float32) * weight[sender, part]
                summed_out[g, part] = r.astype(jnp.bfloat16)
                further[g, p] = send(summed_out.at[g, part], summed_in.at[g, part], there)

        def total(g, p):
            part, sender = parts[p], 4 if low[p] else 3
            directly[g, p].wait_recv()
            r = own[4 * g + 3, part] * weight[2, part] + direct_in[g, part].astype(jnp.float32) * weight[sender, part]
            further[g, p].wait_recv()
            return r + summed_in[g, part].astype(jnp.float32)

        for t in range(3):
            twin_sum(t)
        of_twin.wait_recv()
        mine, other = box[col], twin_line[...]
        top = jnp.maximum(mine, other)
        a, b = jnp.exp2(mine - top), jnp.exp2(other - top)
        weight[0] = jnp.concatenate(spread(a / (a + b)), axis=0)
        weight[1] = jnp.concatenate(spread(b / (a + b)), axis=0)
        own_sum(0)
        own_sum(1)
        own_sum(2)
        first()
        twin_sum(4)
        twin_sum(3)
        twin_sum(5)
        twin_sum(6)
        twin_sum(7)
        own_sum(4)
        own_sum(3)
        own_sum(5)
        own_sum(6)
        settle(box)
        u = -merge(box, float(n_col * cols))
        scale = 1.0 / float(n_col * cols)
        for n, o in ((2, y), (3, y_prev), (4, y_next), (5, y_far)):
            share_of = jnp.exp2(box[col_of(o, zh, 0)] + u) + jnp.exp2(box[col_of(o, zh, 1)] + u)
            weight[n] = jnp.concatenate(spread(share_of * scale), axis=0)
        own_sum(7)
        relay(1)
        for p in ORDER:
            z_out[parts[p]] = first_total(p).astype(jnp.bfloat16)
            over[p] = send(z_out.at[parts[p]], z_in.at[parts[p]], partner)
        direct(1)
        summed(1)
        for i in range(0, rows, LANES):
            s = to_lanes(jnp.sum(noise_sq[i : i + LANES, :], axis=1, keepdims=True), mask)
            row_ref[:, i : i + LANES] = u[:, i : i + LANES] * (EPS / LOG2E) + s / width
        col_ref[...] = col_ref[...] / width + v_line[...] * (EPS / LOG2E)
        for p in ORDER:
            r = total(1, p)
            over[p].wait_recv()
            targets_ref[parts[p]] = (r + z_in[parts[p]].astype(jnp.float32)).astype(jnp.bfloat16)

    gathers()
    updates()
    for ref, n, where in started:
        wait = pltpu.make_async_copy(ref, ref, send_sem.at[n]).wait
        if where is None:
            wait()
        else:
            pl.when(where)(wait)


PARTS = 4
ORDER = (0, 2, 1, 3)
LINE = 180
COPIES = LINE + 4 * PARTS


def body(noise, data):
    rows, part = noise.shape
    cols = data.shape[0]
    width = part * 16
    vmem = pl.BlockSpec(memory_space=pltpu.VMEM)
    bf16, f32 = jnp.bfloat16, jnp.float32
    flops = 2 * 2 * rows * cols * width
    targets, row_potential, col_potential = pl.pallas_call(
        functools.partial(kernel, width),
        out_shape=(
            jax.ShapeDtypeStruct((rows, part), bf16),
            jax.ShapeDtypeStruct((1, rows), f32),
            jax.ShapeDtypeStruct((1, cols), f32),
        ),
        in_specs=[vmem] * 2,
        out_specs=[vmem] * 3,
        scratch_shapes=[
            pltpu.VMEM((16, rows, part), bf16),
            pltpu.VMEM((16, cols, part), bf16),
            pltpu.VMEM((rows, cols), f32),
            pltpu.VMEM((rows, cols), bf16),
            pltpu.VMEM((rows, 1), f32),
            pltpu.VMEM((1, cols), f32),
            pltpu.VMEM((rows, LANES), f32),
            pltpu.VMEM((cols, LANES), f32),
            pltpu.VMEM((ITERS + 1, 16, 1, rows), f32),
            pltpu.VMEM((ITERS, 16, 1, cols), f32),
            pltpu.VMEM((1, rows), f32),
            pltpu.VMEM((8, rows, part), bf16),
            pltpu.VMEM((8, rows, part), bf16),
            pltpu.VMEM((8, rows, part), f32),
            *[pltpu.VMEM((3, rows, part), bf16)] * 2,
            *[pltpu.VMEM((2, rows, part), bf16)] * 6,
            *[pltpu.VMEM((rows, part), bf16)] * 2,
            pltpu.VMEM((6, rows, 1), f32),
            pltpu.SemaphoreType.DMA((COPIES,)),
            pltpu.SemaphoreType.DMA((COPIES,)),
            pltpu.SemaphoreType.DMA((2 * ITERS + 1,)),
            pltpu.SemaphoreType.DMA((2 * ITERS + 1,)),
        ],
        compiler_params=pltpu.CompilerParams(
            collective_id=0,
            has_side_effects=True,
            vmem_limit_bytes=48 * 1024 * 1024,
        ),
        cost_estimate=pl.CostEstimate(
            flops=flops, bytes_accessed=2 * (rows + cols) * part * 2, transcendentals=8 * rows * cols
        ),
    )(noise, data)
    return targets, row_potential.reshape(rows), col_potential.reshape(cols)


def solution(mesh):
    return jax.shard_map(
        body,
        mesh=mesh,
        in_specs=(P("row", "col"), P("col", "row")),
        out_specs=(P("row", "col"), P("row"), P("col")),
        check_vma=False,
    )
```

```python
import functools
import math

import jax
import jax.numpy as jnp
from jax import lax
from jax.experimental import pallas as pl
from jax.experimental.pallas import tpu as pltpu
from jax.sharding import PartitionSpec as P

ITERS = 3
EPS = 0.01
LOG2E = math.log2(math.e)
MESH = pl.DeviceIdType.MESH
NT = (((1,), (1,)), ((), ()))
LANES = 128


def eye():
    r = lax.broadcasted_iota(jnp.int32, (LANES, LANES), 0)
    c = lax.broadcasted_iota(jnp.int32, (LANES, LANES), 1)
    return r == c


def to_lanes(column, mask):
    return jnp.sum(jnp.where(mask, column, 0.0), axis=0, keepdims=True)


def to_sublanes(line, mask):
    return jnp.sum(jnp.where(mask, line, 0.0), axis=1, keepdims=True)


def kernel(
    width,
    noise_ref,
    data_ref,
    targets_ref,
    row_ref,
    col_ref,
    noise_all,
    data_all,
    scores,
    plan,
    u_col,
    v_line,
    noise_sq,
    data_sq,
    row_box,
    col_box,
    twin_line,
    to_twin,
    from_twin,
    own,
    first_out,
    first_in,
    relay_out,
    relay_in,
    direct_out,
    direct_in,
    summed_out,
    summed_in,
    z_out,
    z_in,
    weight,
    send_sem,
    recv_sem,
    load_sem,
    box_send,
    box_recv,
):
    rows, part = noise_ref.shape
    cols = data_ref.shape[0]
    n_row, n_col = 16, 16
    row, col = lax.axis_index("row"), lax.axis_index("col")
    x, zl = row // 4, row % 4
    y, zh, core = col // 4, (col // 2) % 2, col % 2
    mask = eye()
    started = []

    def row_of(x_, zl_):
        return x_ * 4 + zl_

    def col_of(y_, zh_, core_):
        return (y_ * 2 + zh_) * 2 + core_

    def send(src, dst, to, lands=None, where=None, size=None):
        n = len(started)
        started.append((src if size is None else size, n, where))
        copy = pltpu.make_async_remote_copy(
            src_ref=src,
            dst_ref=dst,
            send_sem=send_sem.at[n],
            recv_sem=recv_sem.at[n if lands is None else lands],
            device_id=to,
            device_id_type=MESH,
        )
        copy.start()
        return copy

    x_next, x_prev = lax.rem(x + 1, 4), lax.rem(x + 3, 4)
    y_next, y_prev = lax.rem(y + 1, 4), lax.rem(y + 3, 4)
    x_far, y_far = lax.rem(x + 2, 4), lax.rem(y + 2, 4)
    aside, across = zl + 1 - 2 * lax.rem(zl, 2), 3 - zl
    source = (zl, aside, 2 - zl // 2, 3 - 3 * (zl // 2))
    middle = (zl == 1) | (zl == 2)
    twin = (row, col_of(y, zh, 1 - core))
    partner = (row, col_of(y, 1 - zh, core))
    right, left = (row_of(x_next, zl), col), (row_of(x_prev, zl), col)
    up, down = (row, col_of(y_next, zh, core)), (row, col_of(y_prev, zh, core))
    y_over = (row, col_of(y_far, zh, core))
    z_aside, z_across = (row_of(x, aside), col), (row_of(x, across), col)

    barrier = pltpu.get_barrier_semaphore()
    greeted = (twin, right, left, up, down, z_aside, z_across, partner)
    for to in greeted:
        pl.semaphore_signal(barrier, inc=1, device_id=to, device_id_type=MESH)
    loads = [
        pltpu.make_async_copy(noise_ref, noise_all.at[col], load_sem.at[0]),
        pltpu.make_async_copy(data_ref, data_all.at[row], load_sem.at[1]),
    ]
    for load in loads:
        load.start()
    scores[...] = jnp.zeros_like(scores)
    noise_sq[...] = jnp.zeros_like(noise_sq)
    data_sq[...] = jnp.zeros_like(data_sq)
    for load in loads:
        load.wait()
    pl.semaphore_wait(barrier, len(greeted))

    def accumulate(k):
        a, b = noise_all[k], data_all[k]
        scores[...] += lax.dot_general(a, b, NT, preferred_element_type=jnp.float32)
        a, b = a.astype(jnp.float32), b.astype(jnp.float32)
        a, b = a * a, b * b
        noise_sq[...] += a[:, :LANES] + a[:, LANES:]
        data_sq[...] += b[:, :LANES] + b[:, LANES:]

    def gathers():
        class Ring:
            def __init__(self, array, step, slot_of, after, before):
                self.array, self.step, self.slot_of = array, step, slot_of
                self.after, self.before = after, before
                self.sent = {}

            def part(self, place, p):
                return self.array.at[self.slot_of(place), pl.ds(p * self.step, self.step)]

            def start(self, p):
                block = self.part(0, p)
                ways = (self.after, self.before) if p < PARTS // 2 else (self.before, self.after)
                self.sent[p] = [send(block, block, to) for to in ways]

            def pass_on(self, p):
                self.sent[p][0].wait_recv()
                place, to = (3, self.after) if p < PARTS // 2 else (1, self.before)
                block = self.part(place, p)
                self.sent[p].append(send(block, block, to))

            def near(self):
                for p in ORDER:
                    self.sent[p][1].wait_recv()

            def far(self):
                for p in ORDER:
                    self.sent[p][2].wait_recv()

        def data_slot(k):
            return lambda i: row_of(lax.rem(x + i, 4), source[k])

        def noise_slot(z_):
            return lambda i: col_of(lax.rem(y + i, 4), z_, core)

        d = [Ring(data_all, cols // PARTS, data_slot(k), right, left) for k in range(4)]
        n = [Ring(noise_all, rows // PARTS, noise_slot(z_), up, down) for z_ in (zh, 1 - zh)]
        twins, crossing = [], {}

        def to_the_twin(ring, *places):
            for i in places:
                block = noise_all.at[ring.slot_of(i)]
                twins.append(send(block, block, twin))

        def z_part(k, p):
            return data_all.at[row_of(x, source[k]), pl.ds(p * (cols // PARTS), cols // PARTS)]

        size = z_part(0, 0)

        def z_send(k, p, to, where=None):
            block = z_part(k, p)
            send(block, block, to, LINE + source[k] * PARTS + p, where, size)

        def z_arrive(k, p):
            block = z_part(k, p)
            pltpu.make_async_copy(block, block, recv_sem.at[LINE + source[k] * PARTS + p]).wait()

            @pl.when(middle)
            def _():
                z_send(k, p, z_across if k == 1 else z_aside, middle)

            d[k].start(p)

        def cross(p):
            block = n[0].part(0, p)
            crossing[p] = send(block, block, partner)

        def cross_arrive(p):
            crossing[p].wait_recv()
            block = n[1].part(0, p)
            n[1].sent[p] = [send(block, block, to) for to in (y_over, up, down)]

        for p in ORDER:
            z_send(0, p, z_aside)
            d[0].start(p)

        @pl.when(middle)
        def _():
            for p in ORDER:
                z_send(0, p, z_across, middle)

        for p in ORDER:
            cross(p)
        for p in ORDER:
            n[0].start(p)
        to_the_twin(n[0], 0)
        for p in ORDER:
            z_arrive(1, p)
            d[0].pass_on(p)
        for p in ORDER:
            n[0].pass_on(p)
        for p in ORDER:
            z_arrive(2, p)
            d[1].pass_on(p)
        n[0].near()
        to_the_twin(n[0], 3, 1)
        n[0].far()
        to_the_twin(n[0], 2)
        for p in ORDER:
            cross_arrive(p)
        to_the_twin(n[1], 0)
        for p in ORDER:
            z_arrive(3, p)
        for p in ORDER:
            d[2].pass_on(p)
        for i, place in ((1, 3), (2, 1), (0, 2)):
            for p in ORDER:
                n[1].sent[p][i].wait_recv()
            to_the_twin(n[1], place)
        for p in ORDER:
            d[3].pass_on(p)
        for t in twins:
            t.wait_recv()

        def add_group(k):
            def one(i, carry):
                accumulate(data_slot(k)(i))
                return carry

            lax.fori_loop(0, 4, one, 0)

        for k in (0, 1, 2):
            d[k].near()
            d[k].far()
            add_group(k)
        accumulate(data_slot(3)(0))
        d[3].near()
        accumulate(data_slot(3)(1))
        accumulate(data_slot(3)(3))
        d[3].far()
        accumulate(data_slot(3)(2))

        unit = LOG2E / (EPS * width)
        for i in range(0, rows, LANES):
            scores[i : i + LANES, :] = scores[i : i + LANES, :] * (2.0 * unit)
        for j in range(0, cols, LANES):
            s = to_lanes(jnp.sum(data_sq[j : j + LANES, :], axis=1, keepdims=True), mask)
            col_ref[:, j : j + LANES] = s
            v_line[:, j : j + LANES] = s * -unit

    def updates():
        def share(box, mine, peer_of):
            def one(d, carry):
                pltpu.make_async_remote_copy(
                    src_ref=box.at[mine],
                    dst_ref=box.at[mine],
                    send_sem=box_send.at[shared[0]],
                    recv_sem=box_recv.at[shared[0]],
                    device_id=peer_of(d),
                    device_id_type=MESH,
                ).start()
                return carry

            lax.fori_loop(1, 16, one, 0)

        def settle(box):
            n = shared[0]
            shared[0] += 1
            many = box.at[pl.ds(0, 15)]
            pltpu.make_async_copy(many, many, box_recv.at[n]).wait()
            pltpu.make_async_copy(many, many, box_send.at[n]).wait()

        shared = [0]

        def row_peer(d):
            return (row, lax.rem(col + d, n_col))

        def col_peer(d):
            return (lax.rem(row + d, n_row), col)

        def merge(box, count):
            lines = box[...]
            top = jnp.max(lines, axis=0)
            total = jnp.sum(jnp.exp2(lines - top[None]), axis=0)
            return top + jnp.log(total / count) * LOG2E

        def row_local(box, last):
            v = v_line[...]
            for i in range(0, rows, LANES):
                s = scores[i : i + LANES, :] + v
                top = jnp.max(s, axis=1, keepdims=True)
                p = jnp.exp2(s - top)
                total = jnp.sum(p, axis=1, keepdims=True)
                if last:
                    plan[i : i + LANES, :] = (p * (1.0 / total)).astype(jnp.bfloat16)
                box[col, :, i : i + LANES] = to_lanes(top + jnp.log(total) * LOG2E, mask)

        def row_finish(box):
            u = -merge(box, float(n_col * cols))
            for i in range(0, rows, LANES):
                u_col[i : i + LANES, :] = to_sublanes(u[:, i : i + LANES], mask)

        def col_local(box):
            u = u_col[...]
            for j in range(0, cols, LANES):
                s = scores[:, j : j + LANES] + u
                top = jnp.max(s, axis=0, keepdims=True)
                total = jnp.sum(jnp.exp2(s - top), axis=0, keepdims=True)
                box[row, :, j : j + LANES] = top + jnp.log(total) * LOG2E

        for step in range(ITERS):
            box = row_box.at[step]
            row_local(box, False)
            share(box, col, row_peer)
            settle(box)
            row_finish(box)
            box = col_box.at[step]
            col_local(box)
            share(box, row, col_peer)
            settle(box)
            v_line[...] = -merge(box, float(n_row * rows))
        box = row_box.at[ITERS]
        row_local(box, True)
        of_twin = send(box.at[col], twin_line, twin)
        share(box, col, row_peer)

        def product(k):
            return jnp.dot(plan[...], data_all[k], preferred_element_type=jnp.float32)

        def spread(line):
            return [to_sublanes(line[:, i : i + LANES], mask) for i in range(0, rows, LANES)]

        order = [(o, z_) for z_ in (1 - zh, zh) for o in (y_far, y_next, y_prev, y)]
        give = {}

        def twin_sum(t):
            o, z_ = order[t]
            to_twin[t] = product(col_of(o, z_, 1 - core)).astype(jnp.bfloat16)
            give[t] = send(to_twin.at[t], from_twin.at[t], twin)

        def own_sum(t):
            o, z_ = order[t]
            r = product(col_of(o, z_, core)) * weight[0]
            give[t].wait_recv()
            own[t] = r + from_twin[t].astype(jnp.float32) * weight[1]

        step = rows // PARTS
        parts = [pl.ds(p * step, step) for p in range(PARTS)]
        low = [p < PARTS // 2 for p in range(PARTS)]
        relayed, directly, further, over, straight = {}, {}, {}, {}, {}

        def first():
            for p in ORDER:
                for i, there in enumerate(((row, col_of(y_far, zh, core)), up, down)):
                    first_out[i, parts[p]] = own[i, parts[p]].astype(jnp.bfloat16)
                    straight[i, p] = send(first_out.at[i, parts[p]], first_in.at[i, parts[p]], there)

        def first_total(p):
            part = parts[p]
            r = own[3, part] * weight[2, part]
            for i, sender in ((0, 5), (1, 3), (2, 4)):
                straight[i, p].wait_recv()
                r += first_in[i, part].astype(jnp.float32) * weight[sender, part]
            return r

        def relay(g):
            relay_out[g] = own[4 * g].astype(jnp.bfloat16)
            for p in ORDER:
                there = up if low[p] else down
                relayed[g, p] = send(relay_out.at[g, parts[p]], relay_in.at[g, parts[p]], there)

        def direct(g):
            for p in ORDER:
                t, there = (4 * g + 2, down) if low[p] else (4 * g + 1, up)
                direct_out[g, parts[p]] = own[t, parts[p]].astype(jnp.bfloat16)
                directly[g, p] = send(direct_out.at[g, parts[p]], direct_in.at[g, parts[p]], there)

        def summed(g):
            for p in ORDER:
                t, there, sender = (4 * g + 1, up, 3) if low[p] else (4 * g + 2, down, 4)
                relayed[g, p].wait_recv()
                part = parts[p]
                r = own[t, part] * weight[2, part] + relay_in[g, part].astype(jnp.float32) * weight[sender, part]
                summed_out[g, part] = r.astype(jnp.bfloat16)
                further[g, p] = send(summed_out.at[g, part], summed_in.at[g, part], there)

        def total(g, p):
            part, sender = parts[p], 4 if low[p] else 3
            directly[g, p].wait_recv()
            r = own[4 * g + 3, part] * weight[2, part] + direct_in[g, part].astype(jnp.float32) * weight[sender, part]
            further[g, p].wait_recv()
            return r + summed_in[g, part].astype(jnp.float32)

        for t in range(3):
            twin_sum(t)
        of_twin.wait_recv()
        mine, other = box[col], twin_line[...]
        top = jnp.maximum(mine, other)
        a, b = jnp.exp2(mine - top), jnp.exp2(other - top)
        weight[0] = jnp.concatenate(spread(a / (a + b)), axis=0)
        weight[1] = jnp.concatenate(spread(b / (a + b)), axis=0)
        own_sum(0)
        own_sum(1)
        own_sum(2)
        first()
        twin_sum(4)
        twin_sum(3)
        twin_sum(5)
        twin_sum(6)
        twin_sum(7)
        own_sum(4)
        own_sum(3)
        own_sum(5)
        own_sum(6)
        settle(box)
        u = -merge(box, float(n_col * cols))
        scale = 1.0 / float(n_col * cols)
        for n, o in ((2, y), (3, y_prev), (4, y_next), (5, y_far)):
            share_of = jnp.exp2(box[col_of(o, zh, 0)] + u) + jnp.exp2(box[col_of(o, zh, 1)] + u)
            weight[n] = jnp.concatenate(spread(share_of * scale), axis=0)
        own_sum(7)
        relay(1)
        for p in ORDER:
            z_out[parts[p]] = first_total(p).astype(jnp.bfloat16)
            over[p] = send(z_out.at[parts[p]], z_in.at[parts[p]], partner)
        direct(1)
        summed(1)
        for i in range(0, rows, LANES):
            s = to_lanes(jnp.sum(noise_sq[i : i + LANES, :], axis=1, keepdims=True), mask)
            row_ref[:, i : i + LANES] = u[:, i : i + LANES] * (EPS / LOG2E) + s / width
        col_ref[...] = col_ref[...] / width + v_line[...] * (EPS / LOG2E)
        for p in ORDER:
            r = total(1, p)
            over[p].wait_recv()
            targets_ref[parts[p]] = (r + z_in[parts[p]].astype(jnp.float32)).astype(jnp.bfloat16)

    gathers()
    updates()
    for ref, n, where in started:
        wait = pltpu.make_async_copy(ref, ref, send_sem.at[n]).wait
        if where is None:
            wait()
        else:
            pl.when(where)(wait)


PARTS = 4
ORDER = (0, 2, 1, 3)
LINE = 180
COPIES = LINE + 4 * PARTS


def body(noise, data):
    rows, part = noise.shape
    cols = data.shape[0]
    width = part * 16
    vmem = pl.BlockSpec(memory_space=pltpu.VMEM)
    bf16, f32 = jnp.bfloat16, jnp.float32
    flops = 2 * 2 * rows * cols * width
    targets, row_potential, col_potential = pl.pallas_call(
        functools.partial(kernel, width),
        out_shape=(
            jax.ShapeDtypeStruct((rows, part), bf16),
            jax.ShapeDtypeStruct((1, rows), f32),
            jax.ShapeDtypeStruct((1, cols), f32),
        ),
        in_specs=[pl.BlockSpec(memory_space=pl.ANY)] * 2,
        out_specs=[vmem] * 3,
        scratch_shapes=[
            pltpu.VMEM((16, rows, part), bf16),
            pltpu.VMEM((16, cols, part), bf16),
            pltpu.VMEM((rows, cols), f32),
            pltpu.VMEM((rows, cols), bf16),
            pltpu.VMEM((rows, 1), f32),
            pltpu.VMEM((1, cols), f32),
            pltpu.VMEM((rows, LANES), f32),
            pltpu.VMEM((cols, LANES), f32),
            pltpu.VMEM((ITERS + 1, 16, 1, rows), f32),
            pltpu.VMEM((ITERS, 16, 1, cols), f32),
            pltpu.VMEM((1, rows), f32),
            pltpu.VMEM((8, rows, part), bf16),
            pltpu.VMEM((8, rows, part), bf16),
            pltpu.VMEM((8, rows, part), f32),
            *[pltpu.VMEM((3, rows, part), bf16)] * 2,
            *[pltpu.VMEM((2, rows, part), bf16)] * 6,
            *[pltpu.VMEM((rows, part), bf16)] * 2,
            pltpu.VMEM((6, rows, 1), f32),
            pltpu.SemaphoreType.DMA((COPIES,)),
            pltpu.SemaphoreType.DMA((COPIES,)),
            pltpu.SemaphoreType.DMA((2,)),
            pltpu.SemaphoreType.DMA((2 * ITERS + 1,)),
            pltpu.SemaphoreType.DMA((2 * ITERS + 1,)),
        ],
        compiler_params=pltpu.CompilerParams(
            collective_id=0,
            has_side_effects=True,
            vmem_limit_bytes=54912 * 1024,
        ),
        cost_estimate=pl.CostEstimate(
            flops=flops, bytes_accessed=2 * (rows + cols) * part * 2, transcendentals=8 * rows * cols
        ),
    )(noise, data)
    return targets, row_potential.reshape(rows), col_potential.reshape(cols)


def solution(mesh):
    return jax.shard_map(
        body,
        mesh=mesh,
        in_specs=(P("row", "col"), P("col", "row")),
        out_specs=(P("row", "col"), P("row"), P("col")),
        check_vma=False,
    )
```

```python
import functools
import math

import jax
import jax.numpy as jnp
from jax import lax
from jax.experimental import pallas as pl
from jax.experimental.pallas import tpu as pltpu
from jax.sharding import PartitionSpec as P

ITERS = 3
EPS = 0.01
LOG2E = math.log2(math.e)
MESH = pl.DeviceIdType.MESH
NT = (((1,), (1,)), ((), ()))
LANES = 128


def eye():
    r = lax.broadcasted_iota(jnp.int32, (LANES, LANES), 0)
    c = lax.broadcasted_iota(jnp.int32, (LANES, LANES), 1)
    return r == c


def to_lanes(column, mask):
    return jnp.sum(jnp.where(mask, column, 0.0), axis=0, keepdims=True)


def to_sublanes(line, mask):
    return jnp.sum(jnp.where(mask, line, 0.0), axis=1, keepdims=True)


def kernel(
    width,
    noise_ref,
    data_ref,
    targets_ref,
    row_ref,
    col_ref,
    noise_all,
    data_all,
    scores,
    plan,
    u_col,
    v_line,
    noise_sq,
    data_sq,
    row_box,
    col_box,
    twin_line,
    to_twin,
    from_twin,
    own,
    first_out,
    first_in,
    relay_out,
    relay_in,
    direct_out,
    direct_in,
    summed_out,
    summed_in,
    z_out,
    z_in,
    weight,
    send_sem,
    recv_sem,
    load_sem,
    box_send,
    box_recv,
):
    rows, part = noise_ref.shape
    cols = data_ref.shape[0]
    n_row, n_col = 16, 16
    row, col = lax.axis_index("row"), lax.axis_index("col")
    x, zl = row // 4, row % 4
    y, zh, core = col // 4, (col // 2) % 2, col % 2
    mask = eye()
    started = []

    def row_of(x_, zl_):
        return x_ * 4 + zl_

    def col_of(y_, zh_, core_):
        return (y_ * 2 + zh_) * 2 + core_

    def send(src, dst, to, lands=None, where=None, size=None):
        n = len(started)
        started.append((src if size is None else size, n, where))
        copy = pltpu.make_async_remote_copy(
            src_ref=src,
            dst_ref=dst,
            send_sem=send_sem.at[n],
            recv_sem=recv_sem.at[n if lands is None else lands],
            device_id=to,
            device_id_type=MESH,
        )
        copy.start()
        return copy

    x_next, x_prev = lax.rem(x + 1, 4), lax.rem(x + 3, 4)
    y_next, y_prev = lax.rem(y + 1, 4), lax.rem(y + 3, 4)
    x_far, y_far = lax.rem(x + 2, 4), lax.rem(y + 2, 4)
    aside, across = zl + 1 - 2 * lax.rem(zl, 2), 3 - zl
    source = (zl, aside, 2 - zl // 2, 3 - 3 * (zl // 2))
    middle = (zl == 1) | (zl == 2)
    twin = (row, col_of(y, zh, 1 - core))
    partner = (row, col_of(y, 1 - zh, core))
    right, left = (row_of(x_next, zl), col), (row_of(x_prev, zl), col)
    up, down = (row, col_of(y_next, zh, core)), (row, col_of(y_prev, zh, core))
    y_over = (row, col_of(y_far, zh, core))
    z_aside, z_across = (row_of(x, aside), col), (row_of(x, across), col)

    barrier = pltpu.get_barrier_semaphore()
    greeted = (twin, right, left, up, down, z_aside, z_across, partner)
    for to in greeted:
        pl.semaphore_signal(barrier, inc=1, device_id=to, device_id_type=MESH)
    loads = [
        pltpu.make_async_copy(noise_ref, noise_all.at[col], load_sem.at[0]),
        pltpu.make_async_copy(data_ref, data_all.at[row], load_sem.at[1]),
    ]
    for load in loads:
        load.start()
    scores[...] = jnp.zeros_like(scores)
    noise_sq[...] = jnp.zeros_like(noise_sq)
    data_sq[...] = jnp.zeros_like(data_sq)
    for load in loads:
        load.wait()
    pl.semaphore_wait(barrier, len(greeted))

    def accumulate(k):
        a, b = noise_all[k], data_all[k]
        scores[...] += lax.dot_general(a, b, NT, preferred_element_type=jnp.float32)
        a, b = a.astype(jnp.float32), b.astype(jnp.float32)
        a, b = a * a, b * b
        noise_sq[...] += a[:, :LANES] + a[:, LANES:]
        data_sq[...] += b[:, :LANES] + b[:, LANES:]

    def gathers():
        class Ring:
            def __init__(self, array, step, slot_of, after, before):
                self.array, self.step, self.slot_of = array, step, slot_of
                self.after, self.before = after, before
                self.sent = {}

            def part(self, place, p):
                return self.array.at[self.slot_of(place), pl.ds(p * self.step, self.step)]

            def start(self, p):
                block = self.part(0, p)
                ways = (self.after, self.before) if p < PARTS // 2 else (self.before, self.after)
                self.sent[p] = [send(block, block, to) for to in ways]

            def pass_on(self, p):
                self.sent[p][0].wait_recv()
                place, to = (3, self.after) if p < PARTS // 2 else (1, self.before)
                block = self.part(place, p)
                self.sent[p].append(send(block, block, to))

            def near(self):
                for p in ORDER:
                    self.sent[p][1].wait_recv()

            def far(self):
                for p in ORDER:
                    self.sent[p][2].wait_recv()

        def data_slot(k):
            return lambda i: row_of(lax.rem(x + i, 4), source[k])

        def noise_slot(z_):
            return lambda i: col_of(lax.rem(y + i, 4), z_, core)

        d = [Ring(data_all, cols // PARTS, data_slot(k), right, left) for k in range(4)]
        n = [Ring(noise_all, rows // PARTS, noise_slot(z_), up, down) for z_ in (zh, 1 - zh)]
        twins, crossing = [], {}

        def to_the_twin(ring, *places):
            for i in places:
                block = noise_all.at[ring.slot_of(i)]
                twins.append(send(block, block, twin))

        def z_part(k, p):
            return data_all.at[row_of(x, source[k]), pl.ds(p * (cols // PARTS), cols // PARTS)]

        size = z_part(0, 0)

        def z_send(k, p, to, where=None):
            block = z_part(k, p)
            send(block, block, to, LINE + source[k] * PARTS + p, where, size)

        def z_arrive(k, p):
            block = z_part(k, p)
            pltpu.make_async_copy(block, block, recv_sem.at[LINE + source[k] * PARTS + p]).wait()

            @pl.when(middle)
            def _():
                z_send(k, p, z_across if k == 1 else z_aside, middle)

            d[k].start(p)

        def cross(p):
            block = n[0].part(0, p)
            crossing[p] = send(block, block, partner)

        def cross_arrive(p):
            crossing[p].wait_recv()
            block = n[1].part(0, p)
            n[1].sent[p] = [send(block, block, to) for to in (y_over, up, down)]

        for p in ORDER:
            z_send(0, p, z_aside)
            d[0].start(p)

        @pl.when(middle)
        def _():
            for p in ORDER:
                z_send(0, p, z_across, middle)

        for p in ORDER:
            cross(p)
        for p in ORDER:
            n[0].start(p)
        to_the_twin(n[0], 0)
        for p in ORDER:
            z_arrive(1, p)
            d[0].pass_on(p)
        for p in ORDER:
            n[0].pass_on(p)
        for p in ORDER:
            z_arrive(2, p)
            d[1].pass_on(p)
        n[0].near()
        to_the_twin(n[0], 3, 1)
        n[0].far()
        to_the_twin(n[0], 2)
        for p in ORDER:
            cross_arrive(p)
        to_the_twin(n[1], 0)
        for p in ORDER:
            z_arrive(3, p)
        for p in ORDER:
            d[2].pass_on(p)
        for p in ORDER[:2]:
            d[3].pass_on(p)
        for i, place in ((1, 3), (2, 1), (0, 2)):
            for p in ORDER:
                n[1].sent[p][i].wait_recv()
            to_the_twin(n[1], place)
        for p in ORDER[2:]:
            d[3].pass_on(p)
        for t in twins:
            t.wait_recv()

        def add_group(k):
            def one(i, carry):
                accumulate(data_slot(k)(i))
                return carry

            lax.fori_loop(0, 4, one, 0)

        for k in (0, 1, 2):
            d[k].near()
            d[k].far()
            add_group(k)
        accumulate(data_slot(3)(0))
        d[3].near()
        accumulate(data_slot(3)(1))
        accumulate(data_slot(3)(3))
        d[3].far()
        accumulate(data_slot(3)(2))

        unit = LOG2E / (EPS * width)
        for i in range(0, rows, LANES):
            scores[i : i + LANES, :] = scores[i : i + LANES, :] * (2.0 * unit)
        for j in range(0, cols, LANES):
            s = to_lanes(jnp.sum(data_sq[j : j + LANES, :], axis=1, keepdims=True), mask)
            col_ref[:, j : j + LANES] = s
            v_line[:, j : j + LANES] = s * -unit

    def updates():
        def share(box, mine, peers):
            def one(d, carry):
                pltpu.make_async_remote_copy(
                    src_ref=box.at[mine],
                    dst_ref=box.at[mine],
                    send_sem=box_send.at[shared[0]],
                    recv_sem=box_recv.at[shared[0]],
                    device_id=d,
                    device_id_type=MESH,
                ).start()
                return carry

            for peer in peers:
                one(peer, 0)

        def settle(box):
            n = shared[0]
            shared[0] += 1
            many = box.at[pl.ds(0, 15)]
            pltpu.make_async_copy(many, many, box_recv.at[n]).wait()
            pltpu.make_async_copy(many, many, box_send.at[n]).wait()

        shared = [0]

        row_peer = [
            (row, col_of(lax.rem(y + o, 4), z_, c)) for z_ in (1 - zh, zh) for o in (2, 1, 3) for c in (core, 1 - core)
        ]
        row_peer += [(row, col_of(y, z_, c)) for z_, c in ((1 - zh, core), (1 - zh, 1 - core), (zh, 1 - core))]
        col_peer = [
            (row_of(lax.rem(x + o, 4), z_), col) for z_ in (across, lax.rem(zl + 2, 4), aside) for o in (2, 1, 3, 0)
        ]
        col_peer += [(row_of(lax.rem(x + o, 4), zl), col) for o in (2, 1, 3)]

        def merge(box, count):
            lines = box[...]
            top = jnp.max(lines, axis=0)
            total = jnp.sum(jnp.exp2(lines - top[None]), axis=0)
            return top + jnp.log(total / count) * LOG2E

        def row_local(box, last):
            v = v_line[...]
            for i in range(0, rows, LANES):
                s = scores[i : i + LANES, :] + v
                top = jnp.max(s, axis=1, keepdims=True)
                p = jnp.exp2(s - top)
                total = jnp.sum(p, axis=1, keepdims=True)
                if last:
                    plan[i : i + LANES, :] = (p * (1.0 / total)).astype(jnp.bfloat16)
                box[col, :, i : i + LANES] = to_lanes(top + jnp.log(total) * LOG2E, mask)

        def row_finish(box):
            u = -merge(box, float(n_col * cols))
            for i in range(0, rows, LANES):
                u_col[i : i + LANES, :] = to_sublanes(u[:, i : i + LANES], mask)

        def col_local(box):
            u = u_col[...]
            for j in range(0, cols, LANES):
                s = scores[:, j : j + LANES] + u
                top = jnp.max(s, axis=0, keepdims=True)
                total = jnp.sum(jnp.exp2(s - top), axis=0, keepdims=True)
                box[row, :, j : j + LANES] = top + jnp.log(total) * LOG2E

        for step in range(ITERS):
            box = row_box.at[step]
            row_local(box, False)
            share(box, col, row_peer)
            settle(box)
            row_finish(box)
            box = col_box.at[step]
            col_local(box)
            share(box, row, col_peer)
            settle(box)
            v_line[...] = -merge(box, float(n_row * rows))
        box = row_box.at[ITERS]
        row_local(box, True)
        of_twin = send(box.at[col], twin_line, twin)
        share(box, col, row_peer)

        def product(k):
            return jnp.dot(plan[...], data_all[k], preferred_element_type=jnp.float32)

        def spread(line):
            return [to_sublanes(line[:, i : i + LANES], mask) for i in range(0, rows, LANES)]

        order = [(o, z_) for z_ in (1 - zh, zh) for o in (y_far, y_next, y_prev, y)]
        give = {}

        def twin_sum(t):
            o, z_ = order[t]
            to_twin[t] = product(col_of(o, z_, 1 - core)).astype(jnp.bfloat16)
            give[t] = send(to_twin.at[t], from_twin.at[t], twin)

        def own_sum(t):
            o, z_ = order[t]
            r = product(col_of(o, z_, core)) * weight[0]
            give[t].wait_recv()
            own[t] = r + from_twin[t].astype(jnp.float32) * weight[1]

        step = rows // PARTS
        parts = [pl.ds(p * step, step) for p in range(PARTS)]
        low = [p < PARTS // 2 for p in range(PARTS)]
        relayed, directly, further, over, straight = {}, {}, {}, {}, {}

        def first():
            for p in ORDER:
                for i, there in enumerate(((row, col_of(y_far, zh, core)), up, down)):
                    first_out[i, parts[p]] = own[i, parts[p]].astype(jnp.bfloat16)
                    straight[i, p] = send(first_out.at[i, parts[p]], first_in.at[i, parts[p]], there)

        def first_total(p):
            part = parts[p]
            r = own[3, part] * weight[2, part]
            for i, sender in ((0, 5), (1, 3), (2, 4)):
                straight[i, p].wait_recv()
                r += first_in[i, part].astype(jnp.float32) * weight[sender, part]
            return r

        def relay(g):
            relay_out[g] = own[4 * g].astype(jnp.bfloat16)
            for p in ORDER:
                there = up if low[p] else down
                relayed[g, p] = send(relay_out.at[g, parts[p]], relay_in.at[g, parts[p]], there)

        def direct(g):
            for p in ORDER:
                t, there = (4 * g + 2, down) if low[p] else (4 * g + 1, up)
                direct_out[g, parts[p]] = own[t, parts[p]].astype(jnp.bfloat16)
                directly[g, p] = send(direct_out.at[g, parts[p]], direct_in.at[g, parts[p]], there)

        def summed(g):
            for p in ORDER:
                t, there, sender = (4 * g + 1, up, 3) if low[p] else (4 * g + 2, down, 4)
                relayed[g, p].wait_recv()
                part = parts[p]
                r = own[t, part] * weight[2, part] + relay_in[g, part].astype(jnp.float32) * weight[sender, part]
                summed_out[g, part] = r.astype(jnp.bfloat16)
                further[g, p] = send(summed_out.at[g, part], summed_in.at[g, part], there)

        def total(g, p):
            part, sender = parts[p], 4 if low[p] else 3
            directly[g, p].wait_recv()
            r = own[4 * g + 3, part] * weight[2, part] + direct_in[g, part].astype(jnp.float32) * weight[sender, part]
            further[g, p].wait_recv()
            return r + summed_in[g, part].astype(jnp.float32)

        for t in range(3):
            twin_sum(t)
        of_twin.wait_recv()
        mine, other = box[col], twin_line[...]
        top = jnp.maximum(mine, other)
        a, b = jnp.exp2(mine - top), jnp.exp2(other - top)
        weight[0] = jnp.concatenate(spread(a / (a + b)), axis=0)
        weight[1] = jnp.concatenate(spread(b / (a + b)), axis=0)
        own_sum(0)
        own_sum(1)
        own_sum(2)
        first()
        twin_sum(4)
        twin_sum(3)
        twin_sum(5)
        twin_sum(6)
        twin_sum(7)
        own_sum(4)
        own_sum(3)
        own_sum(5)
        own_sum(6)
        settle(box)
        u = -merge(box, float(n_col * cols))
        scale = 1.0 / float(n_col * cols)
        for n, o in ((2, y), (3, y_prev), (4, y_next), (5, y_far)):
            share_of = jnp.exp2(box[col_of(o, zh, 0)] + u) + jnp.exp2(box[col_of(o, zh, 1)] + u)
            weight[n] = jnp.concatenate(spread(share_of * scale), axis=0)
        own_sum(7)
        relay(1)
        for p in ORDER:
            z_out[parts[p]] = first_total(p).astype(jnp.bfloat16)
            over[p] = send(z_out.at[parts[p]], z_in.at[parts[p]], partner)
        direct(1)
        summed(1)
        for i in range(0, rows, LANES):
            s = to_lanes(jnp.sum(noise_sq[i : i + LANES, :], axis=1, keepdims=True), mask)
            row_ref[:, i : i + LANES] = u[:, i : i + LANES] * (EPS / LOG2E) + s / width
        col_ref[...] = col_ref[...] / width + v_line[...] * (EPS / LOG2E)
        for p in ORDER:
            r = total(1, p)
            over[p].wait_recv()
            targets_ref[parts[p]] = (r + z_in[parts[p]].astype(jnp.float32)).astype(jnp.bfloat16)

    gathers()
    updates()
    for ref, n, where in started:
        wait = pltpu.make_async_copy(ref, ref, send_sem.at[n]).wait
        if where is None:
            wait()
        else:
            pl.when(where)(wait)


PARTS = 4
ORDER = (0, 2, 1, 3)
LINE = 180
COPIES = LINE + 4 * PARTS


def body(noise, data):
    rows, part = noise.shape
    cols = data.shape[0]
    width = part * 16
    vmem = pl.BlockSpec(memory_space=pltpu.VMEM)
    bf16, f32 = jnp.bfloat16, jnp.float32
    flops = 2 * 2 * rows * cols * width
    targets, row_potential, col_potential = pl.pallas_call(
        functools.partial(kernel, width),
        out_shape=(
            jax.ShapeDtypeStruct((rows, part), bf16),
            jax.ShapeDtypeStruct((1, rows), f32),
            jax.ShapeDtypeStruct((1, cols), f32),
        ),
        in_specs=[pl.BlockSpec(memory_space=pl.ANY)] * 2,
        out_specs=[vmem] * 3,
        scratch_shapes=[
            pltpu.VMEM((16, rows, part), bf16),
            pltpu.VMEM((16, cols, part), bf16),
            pltpu.VMEM((rows, cols), f32),
            pltpu.VMEM((rows, cols), bf16),
            pltpu.VMEM((rows, 1), f32),
            pltpu.VMEM((1, cols), f32),
            pltpu.VMEM((rows, LANES), f32),
            pltpu.VMEM((cols, LANES), f32),
            pltpu.VMEM((ITERS + 1, 16, 1, rows), f32),
            pltpu.VMEM((ITERS, 16, 1, cols), f32),
            pltpu.VMEM((1, rows), f32),
            pltpu.VMEM((8, rows, part), bf16),
            pltpu.VMEM((8, rows, part), bf16),
            pltpu.VMEM((8, rows, part), f32),
            *[pltpu.VMEM((3, rows, part), bf16)] * 2,
            *[pltpu.VMEM((2, rows, part), bf16)] * 6,
            *[pltpu.VMEM((rows, part), bf16)] * 2,
            pltpu.VMEM((6, rows, 1), f32),
            pltpu.SemaphoreType.DMA((COPIES,)),
            pltpu.SemaphoreType.DMA((COPIES,)),
            pltpu.SemaphoreType.DMA((2,)),
            pltpu.SemaphoreType.DMA((2 * ITERS + 1,)),
            pltpu.SemaphoreType.DMA((2 * ITERS + 1,)),
        ],
        compiler_params=pltpu.CompilerParams(
            collective_id=0,
            has_side_effects=True,
            vmem_limit_bytes=54912 * 1024,
        ),
        cost_estimate=pl.CostEstimate(
            flops=flops, bytes_accessed=2 * (rows + cols) * part * 2, transcendentals=8 * rows * cols
        ),
    )(noise, data)
    return targets, row_potential.reshape(rows), col_potential.reshape(cols)


def solution(mesh):
    return jax.shard_map(
        body,
        mesh=mesh,
        in_specs=(P("row", "col"), P("col", "row")),
        out_specs=(P("row", "col"), P("row"), P("col")),
        check_vma=False,
    )
```

```python
import functools
import math

import jax
import jax.numpy as jnp
from jax import lax
from jax.experimental import pallas as pl
from jax.experimental.pallas import tpu as pltpu
from jax.sharding import PartitionSpec as P

ITERS = 3
EPS = 0.01
LOG2E = math.log2(math.e)
MESH = pl.DeviceIdType.MESH
NT = (((1,), (1,)), ((), ()))
LANES = 128


def eye():
    r = lax.broadcasted_iota(jnp.int32, (LANES, LANES), 0)
    c = lax.broadcasted_iota(jnp.int32, (LANES, LANES), 1)
    return r == c


def to_lanes(column, mask):
    return jnp.sum(jnp.where(mask, column, 0.0), axis=0, keepdims=True)


def to_sublanes(line, mask):
    return jnp.sum(jnp.where(mask, line, 0.0), axis=1, keepdims=True)


def kernel(
    width,
    noise_ref,
    data_ref,
    targets_ref,
    row_ref,
    col_ref,
    noise_all,
    data_all,
    scores,
    plan,
    u_col,
    v_line,
    noise_sq,
    data_sq,
    row_box,
    col_box,
    twin_line,
    to_twin,
    from_twin,
    own,
    first_out,
    first_in,
    relay_out,
    relay_in,
    direct_out,
    direct_in,
    summed_out,
    summed_in,
    z_out,
    z_in,
    weight,
    send_sem,
    recv_sem,
    load_sem,
    box_send,
    box_recv,
):
    rows, part = noise_ref.shape
    cols = data_ref.shape[0]
    n_row, n_col = 16, 16
    row, col = lax.axis_index("row"), lax.axis_index("col")
    x, zl = row // 4, row % 4
    y, zh, core = col // 4, (col // 2) % 2, col % 2
    mask = eye()
    started = []

    def row_of(x_, zl_):
        return x_ * 4 + zl_

    def col_of(y_, zh_, core_):
        return (y_ * 2 + zh_) * 2 + core_

    def send(src, dst, to, lands=None, where=None, size=None):
        n = len(started)
        started.append((src if size is None else size, n, where))
        copy = pltpu.make_async_remote_copy(
            src_ref=src,
            dst_ref=dst,
            send_sem=send_sem.at[n],
            recv_sem=recv_sem.at[n if lands is None else lands],
            device_id=to,
            device_id_type=MESH,
        )
        copy.start()
        return copy

    x_next, x_prev = lax.rem(x + 1, 4), lax.rem(x + 3, 4)
    y_next, y_prev = lax.rem(y + 1, 4), lax.rem(y + 3, 4)
    x_far, y_far = lax.rem(x + 2, 4), lax.rem(y + 2, 4)
    aside, across = zl + 1 - 2 * lax.rem(zl, 2), 3 - zl
    source = (zl, aside, 2 - zl // 2, 3 - 3 * (zl // 2))
    middle = (zl == 1) | (zl == 2)
    twin = (row, col_of(y, zh, 1 - core))
    partner = (row, col_of(y, 1 - zh, core))
    right, left = (row_of(x_next, zl), col), (row_of(x_prev, zl), col)
    up, down = (row, col_of(y_next, zh, core)), (row, col_of(y_prev, zh, core))
    y_over = (row, col_of(y_far, zh, core))
    z_aside, z_across = (row_of(x, aside), col), (row_of(x, across), col)

    barrier = pltpu.get_barrier_semaphore()
    greeted = (twin, right, left, up, down, z_aside, z_across, partner)
    for to in greeted:
        pl.semaphore_signal(barrier, inc=1, device_id=to, device_id_type=MESH)
    loads = [
        pltpu.make_async_copy(noise_ref, noise_all.at[col], load_sem.at[0]),
        pltpu.make_async_copy(data_ref, data_all.at[row], load_sem.at[1]),
    ]
    for load in loads:
        load.start()
    scores[...] = jnp.zeros_like(scores)
    noise_sq[...] = jnp.zeros_like(noise_sq)
    data_sq[...] = jnp.zeros_like(data_sq)
    for load in loads:
        load.wait()
    pl.semaphore_wait(barrier, len(greeted))

    unit = LOG2E / (EPS * width)

    def accumulate(k, factor=None):
        a, b = noise_all[k], data_all[k]
        r = scores[...] + lax.dot_general(a, b, NT, preferred_element_type=jnp.float32)
        scores[...] = r if factor is None else r * factor
        a, b = a.astype(jnp.float32), b.astype(jnp.float32)
        a, b = a * a, b * b
        noise_sq[...] += a[:, :LANES] + a[:, LANES:]
        data_sq[...] += b[:, :LANES] + b[:, LANES:]

    def gathers():
        class Ring:
            def __init__(self, array, step, slot_of, after, before):
                self.array, self.step, self.slot_of = array, step, slot_of
                self.after, self.before = after, before
                self.sent = {}

            def part(self, place, p):
                return self.array.at[self.slot_of(place), pl.ds(p * self.step, self.step)]

            def start(self, p):
                block = self.part(0, p)
                ways = (self.after, self.before) if p < PARTS // 2 else (self.before, self.after)
                self.sent[p] = [send(block, block, to) for to in ways]

            def pass_on(self, p):
                self.sent[p][0].wait_recv()
                place, to = (3, self.after) if p < PARTS // 2 else (1, self.before)
                block = self.part(place, p)
                self.sent[p].append(send(block, block, to))

            def near(self):
                for p in ORDER:
                    self.sent[p][1].wait_recv()

            def far(self):
                for p in ORDER:
                    self.sent[p][2].wait_recv()

        def data_slot(k):
            return lambda i: row_of(lax.rem(x + i, 4), source[k])

        def noise_slot(z_):
            return lambda i: col_of(lax.rem(y + i, 4), z_, core)

        d = [Ring(data_all, cols // PARTS, data_slot(k), right, left) for k in range(4)]
        n = [Ring(noise_all, rows // PARTS, noise_slot(z_), up, down) for z_ in (zh, 1 - zh)]
        twins, crossing = [], {}

        def to_the_twin(ring, *places):
            for i in places:
                block = noise_all.at[ring.slot_of(i)]
                twins.append(send(block, block, twin))

        def z_part(k, p):
            return data_all.at[row_of(x, source[k]), pl.ds(p * (cols // PARTS), cols // PARTS)]

        size = z_part(0, 0)

        def z_send(k, p, to, where=None):
            block = z_part(k, p)
            send(block, block, to, LINE + source[k] * PARTS + p, where, size)

        def z_arrive(k, p):
            block = z_part(k, p)
            pltpu.make_async_copy(block, block, recv_sem.at[LINE + source[k] * PARTS + p]).wait()

            @pl.when(middle)
            def _():
                z_send(k, p, z_across if k == 1 else z_aside, middle)

            d[k].start(p)

        def cross(p):
            block = n[0].part(0, p)
            crossing[p] = send(block, block, partner)

        def cross_arrive(p):
            crossing[p].wait_recv()
            block = n[1].part(0, p)
            n[1].sent[p] = [send(block, block, to) for to in (y_over, up, down)]

        for p in ORDER:
            z_send(0, p, z_aside)
            d[0].start(p)

        @pl.when(middle)
        def _():
            for p in ORDER:
                z_send(0, p, z_across, middle)

        for p in ORDER:
            cross(p)
        for p in ORDER:
            n[0].start(p)
        to_the_twin(n[0], 0)
        for p in ORDER:
            z_arrive(1, p)
            d[0].pass_on(p)
        for p in ORDER:
            n[0].pass_on(p)
        for p in ORDER:
            z_arrive(2, p)
            d[1].pass_on(p)
        n[0].near()
        to_the_twin(n[0], 3, 1)
        n[0].far()
        to_the_twin(n[0], 2)
        for p in ORDER:
            cross_arrive(p)
        to_the_twin(n[1], 0)
        for p in ORDER:
            z_arrive(3, p)
        for p in ORDER:
            d[2].pass_on(p)
        for p in ORDER[:2]:
            d[3].pass_on(p)
        for i, place in ((1, 3), (2, 1), (0, 2)):
            for p in ORDER:
                n[1].sent[p][i].wait_recv()
            to_the_twin(n[1], place)
        for p in ORDER[2:]:
            d[3].pass_on(p)
        for t in twins:
            t.wait_recv()

        def add_group(k):
            def one(i, carry):
                accumulate(data_slot(k)(i))
                return carry

            lax.fori_loop(0, 4, one, 0)

        for k in (0, 1, 2):
            d[k].near()
            d[k].far()
            add_group(k)
        accumulate(data_slot(3)(0))
        d[3].near()
        accumulate(data_slot(3)(1))
        accumulate(data_slot(3)(3))
        d[3].far()
        accumulate(data_slot(3)(2), 2.0 * unit)

        for j in range(0, cols, LANES):
            s = to_lanes(jnp.sum(data_sq[j : j + LANES, :], axis=1, keepdims=True), mask)
            col_ref[:, j : j + LANES] = s
            v_line[:, j : j + LANES] = s * -unit

    def updates():
        def share(box, mine, peers):
            def one(d, carry):
                pltpu.make_async_remote_copy(
                    src_ref=box.at[mine],
                    dst_ref=box.at[mine],
                    send_sem=box_send.at[shared[0]],
                    recv_sem=box_recv.at[shared[0]],
                    device_id=d,
                    device_id_type=MESH,
                ).start()
                return carry

            for peer in peers:
                one(peer, 0)

        def settle(box):
            n = shared[0]
            shared[0] += 1
            many = box.at[pl.ds(0, 15)]
            pltpu.make_async_copy(many, many, box_recv.at[n]).wait()
            pltpu.make_async_copy(many, many, box_send.at[n]).wait()

        shared = [0]

        row_peer = [
            (row, col_of(lax.rem(y + o, 4), z_, c)) for z_ in (1 - zh, zh) for o in (2, 1, 3) for c in (core, 1 - core)
        ]
        row_peer += [(row, col_of(y, z_, c)) for z_, c in ((1 - zh, core), (1 - zh, 1 - core), (zh, 1 - core))]
        col_peer = [
            (row_of(lax.rem(x + o, 4), z_), col) for z_ in (across, lax.rem(zl + 2, 4), aside) for o in (2, 1, 3, 0)
        ]
        col_peer += [(row_of(lax.rem(x + o, 4), zl), col) for o in (2, 1, 3)]

        def merge(box, count):
            lines = box[...]
            top = jnp.max(lines, axis=0)
            total = jnp.sum(jnp.exp2(lines - top[None]), axis=0)
            return top + jnp.log(total / count) * LOG2E

        def row_local(box, last):
            v = v_line[...]
            for i in range(0, rows, LANES):
                s = scores[i : i + LANES, :] + v
                top = jnp.max(s, axis=1, keepdims=True)
                p = jnp.exp2(s - top)
                total = jnp.sum(p, axis=1, keepdims=True)
                if last:
                    plan[i : i + LANES, :] = (p * (1.0 / total)).astype(jnp.bfloat16)
                box[col, :, i : i + LANES] = to_lanes(top + jnp.log(total) * LOG2E, mask)

        def row_finish(box):
            u = -merge(box, float(n_col * cols))
            for i in range(0, rows, LANES):
                u_col[i : i + LANES, :] = to_sublanes(u[:, i : i + LANES], mask)

        def col_local(box):
            u = u_col[...]
            for j in range(0, cols, LANES):
                s = scores[:, j : j + LANES] + u
                top = jnp.max(s, axis=0, keepdims=True)
                total = jnp.sum(jnp.exp2(s - top), axis=0, keepdims=True)
                box[row, :, j : j + LANES] = top + jnp.log(total) * LOG2E

        for step in range(ITERS):
            box = row_box.at[step]
            row_local(box, False)
            share(box, col, row_peer)
            settle(box)
            row_finish(box)
            box = col_box.at[step]
            col_local(box)
            share(box, row, col_peer)
            settle(box)
            v_line[...] = -merge(box, float(n_row * rows))
        box = row_box.at[ITERS]
        row_local(box, True)
        of_twin = send(box.at[col], twin_line, twin)
        share(box, col, row_peer)

        def product(k):
            return jnp.dot(plan[...], data_all[k], preferred_element_type=jnp.float32)

        def spread(line):
            return [to_sublanes(line[:, i : i + LANES], mask) for i in range(0, rows, LANES)]

        order = [(o, z_) for z_ in (1 - zh, zh) for o in (y_far, y_next, y_prev, y)]
        give = {}

        def twin_sum(t):
            o, z_ = order[t]
            to_twin[t] = product(col_of(o, z_, 1 - core)).astype(jnp.bfloat16)
            give[t] = send(to_twin.at[t], from_twin.at[t], twin)

        def own_sum(t):
            o, z_ = order[t]
            r = product(col_of(o, z_, core)) * weight[0]
            give[t].wait_recv()
            own[t] = r + from_twin[t].astype(jnp.float32) * weight[1]

        step = rows // PARTS
        parts = [pl.ds(p * step, step) for p in range(PARTS)]
        low = [p < PARTS // 2 for p in range(PARTS)]
        relayed, directly, further, over, straight = {}, {}, {}, {}, {}

        def first():
            for p in ORDER:
                for i, there in enumerate(((row, col_of(y_far, zh, core)), up, down)):
                    first_out[i, parts[p]] = own[i, parts[p]].astype(jnp.bfloat16)
                    straight[i, p] = send(first_out.at[i, parts[p]], first_in.at[i, parts[p]], there)

        def first_total(p):
            part = parts[p]
            r = own[3, part] * weight[2, part]
            for i, sender in ((0, 5), (1, 3), (2, 4)):
                straight[i, p].wait_recv()
                r += first_in[i, part].astype(jnp.float32) * weight[sender, part]
            return r

        def relay(g):
            relay_out[g] = own[4 * g].astype(jnp.bfloat16)
            for p in ORDER:
                there = up if low[p] else down
                relayed[g, p] = send(relay_out.at[g, parts[p]], relay_in.at[g, parts[p]], there)

        def direct(g):
            for p in ORDER:
                t, there = (4 * g + 2, down) if low[p] else (4 * g + 1, up)
                direct_out[g, parts[p]] = own[t, parts[p]].astype(jnp.bfloat16)
                directly[g, p] = send(direct_out.at[g, parts[p]], direct_in.at[g, parts[p]], there)

        def summed(g):
            for p in ORDER:
                t, there, sender = (4 * g + 1, up, 3) if low[p] else (4 * g + 2, down, 4)
                relayed[g, p].wait_recv()
                part = parts[p]
                r = own[t, part] * weight[2, part] + relay_in[g, part].astype(jnp.float32) * weight[sender, part]
                summed_out[g, part] = r.astype(jnp.bfloat16)
                further[g, p] = send(summed_out.at[g, part], summed_in.at[g, part], there)

        def total(g, p):
            part, sender = parts[p], 4 if low[p] else 3
            directly[g, p].wait_recv()
            r = own[4 * g + 3, part] * weight[2, part] + direct_in[g, part].astype(jnp.float32) * weight[sender, part]
            further[g, p].wait_recv()
            return r + summed_in[g, part].astype(jnp.float32)

        for t in range(3):
            twin_sum(t)
        of_twin.wait_recv()
        mine, other = box[col], twin_line[...]
        top = jnp.maximum(mine, other)
        a, b = jnp.exp2(mine - top), jnp.exp2(other - top)
        weight[0] = jnp.concatenate(spread(a / (a + b)), axis=0)
        weight[1] = jnp.concatenate(spread(b / (a + b)), axis=0)
        own_sum(0)
        own_sum(1)
        own_sum(2)
        first()
        twin_sum(4)
        twin_sum(3)
        twin_sum(5)
        twin_sum(6)
        twin_sum(7)
        own_sum(4)
        own_sum(3)
        own_sum(5)
        own_sum(6)
        settle(box)
        u = -merge(box, float(n_col * cols))
        scale = 1.0 / float(n_col * cols)
        for n, o in ((2, y), (3, y_prev), (4, y_next), (5, y_far)):
            share_of = jnp.exp2(box[col_of(o, zh, 0)] + u) + jnp.exp2(box[col_of(o, zh, 1)] + u)
            weight[n] = jnp.concatenate(spread(share_of * scale), axis=0)
        own_sum(7)
        relay(1)
        for p in ORDER:
            z_out[parts[p]] = first_total(p).astype(jnp.bfloat16)
            over[p] = send(z_out.at[parts[p]], z_in.at[parts[p]], partner)
        direct(1)
        summed(1)
        for i in range(0, rows, LANES):
            s = to_lanes(jnp.sum(noise_sq[i : i + LANES, :], axis=1, keepdims=True), mask)
            row_ref[:, i : i + LANES] = u[:, i : i + LANES] * (EPS / LOG2E) + s / width
        col_ref[...] = col_ref[...] / width + v_line[...] * (EPS / LOG2E)
        for p in ORDER:
            r = total(1, p)
            over[p].wait_recv()
            targets_ref[parts[p]] = (r + z_in[parts[p]].astype(jnp.float32)).astype(jnp.bfloat16)

    gathers()
    updates()
    for ref, n, where in started:
        wait = pltpu.make_async_copy(ref, ref, send_sem.at[n]).wait
        if where is None:
            wait()
        else:
            pl.when(where)(wait)


PARTS = 4
ORDER = (0, 2, 1, 3)
LINE = 180
COPIES = LINE + 4 * PARTS


def body(noise, data):
    rows, part = noise.shape
    cols = data.shape[0]
    width = part * 16
    vmem = pl.BlockSpec(memory_space=pltpu.VMEM)
    bf16, f32 = jnp.bfloat16, jnp.float32
    flops = 2 * 2 * rows * cols * width
    targets, row_potential, col_potential = pl.pallas_call(
        functools.partial(kernel, width),
        out_shape=(
            jax.ShapeDtypeStruct((rows, part), bf16),
            jax.ShapeDtypeStruct((1, rows), f32),
            jax.ShapeDtypeStruct((1, cols), f32),
        ),
        in_specs=[pl.BlockSpec(memory_space=pl.ANY)] * 2,
        out_specs=[vmem] * 3,
        scratch_shapes=[
            pltpu.VMEM((16, rows, part), bf16),
            pltpu.VMEM((16, cols, part), bf16),
            pltpu.VMEM((rows, cols), f32),
            pltpu.VMEM((rows, cols), bf16),
            pltpu.VMEM((rows, 1), f32),
            pltpu.VMEM((1, cols), f32),
            pltpu.VMEM((rows, LANES), f32),
            pltpu.VMEM((cols, LANES), f32),
            pltpu.VMEM((ITERS + 1, 16, 1, rows), f32),
            pltpu.VMEM((ITERS, 16, 1, cols), f32),
            pltpu.VMEM((1, rows), f32),
            pltpu.VMEM((8, rows, part), bf16),
            pltpu.VMEM((8, rows, part), bf16),
            pltpu.VMEM((8, rows, part), f32),
            *[pltpu.VMEM((3, rows, part), bf16)] * 2,
            *[pltpu.VMEM((2, rows, part), bf16)] * 6,
            *[pltpu.VMEM((rows, part), bf16)] * 2,
            pltpu.VMEM((6, rows, 1), f32),
            pltpu.SemaphoreType.DMA((COPIES,)),
            pltpu.SemaphoreType.DMA((COPIES,)),
            pltpu.SemaphoreType.DMA((2,)),
            pltpu.SemaphoreType.DMA((2 * ITERS + 1,)),
            pltpu.SemaphoreType.DMA((2 * ITERS + 1,)),
        ],
        compiler_params=pltpu.CompilerParams(
            collective_id=0,
            has_side_effects=True,
            vmem_limit_bytes=54912 * 1024,
        ),
        cost_estimate=pl.CostEstimate(
            flops=flops, bytes_accessed=2 * (rows + cols) * part * 2, transcendentals=8 * rows * cols
        ),
    )(noise, data)
    return targets, row_potential.reshape(rows), col_potential.reshape(cols)


def solution(mesh):
    return jax.shard_map(
        body,
        mesh=mesh,
        in_specs=(P("row", "col"), P("col", "row")),
        out_specs=(P("row", "col"), P("row"), P("col")),
        check_vma=False,
    )
```
